512 devices in a mesh: seq: 32 (over z_lo, y, core), head: 16 (over z_hi, x).
Axes of the slice: x: 4, y: 8, z: 8 (z_hi: 4, z_lo: 2; z = z_hi * 2 + z_lo), core: 2. Of those that a mesh axis runs over, the one named last changes fastest.
Arguments:
- source_hidden: bfloat16 [8192, 2048], P('seq', 'head'), may hold values from -64 to 64
- target_hidden: bfloat16 [16384, 2048], P('seq', 'head'), may hold values from -64 to 64
- source_length: int32 [1], replicated, may hold values from 4096 to 8192
- target_length: int32 [1], replicated, may hold values from 8192 to 16384
- encoder_gain: float32 [2048], replicated, may hold values from 0.25 to 1.75
- query_weight: bfloat16 [2048, 2048], P(None, 'head'), may hold values from -1 to 1
- key_weight: bfloat16 [2048, 2048], P(None, 'head'), may hold values from -1 to 1
- value_weight: bfloat16 [2048, 2048], P(None, 'head'), may hold values from -0.5 to 0.5
- output_weight: bfloat16 [2048, 2048], P('head'), may hold values from -0.5 to 0.5
- final_gain: float32 [2048], replicated, may hold values from 0.25 to 1.75
- cross_query: bfloat16 [2048, 2048], P(None, 'head'), may hold values from -1 to 1
- cross_key: bfloat16 [2048, 2048], P(None, 'head'), may hold values from -1 to 1
- cross_value: bfloat16 [2048, 2048], P(None, 'head'), may hold values from -0.5 to 0.5
- cross_gain: float32 [2048], replicated, may hold values from 0.25 to 1.75
Outputs:
- encoder_out: bfloat16 [8192, 2048], P('seq', 'head')
- cross_context: bfloat16 [16384, 2048], P('seq', 'head')
The draws below stay inside these ranges and needn't reach their ends.
All inputs are finite; a program needn't handle non-finite values.
Results may differ from the reference program's by a relative error of at most 0.03.
Values may be sent and summed in bfloat16 or wider, within the bound.
No kernel may reach another device: no remote copies, remote signals or barrier semaphores. Data moves between devices by JAX's collectives and lax.ppermute only.
A program may use at most 64 MiB of HBM per device.

```python
import math
import jax
import jax.numpy as jnp
from jax import lax

HD = 128
H = 16
D = 2048
SRC_LEN = 8192
TGT_LEN = 16384


def shared_direction(key):
    return jnp.clip(jax.random.normal(jax.random.fold_in(key, 901), (D,), jnp.float32), -5.0, 5.0)


def weight_matrix(key, scale, spike, direction):
    base = jnp.clip(jax.random.normal(key, (D, D), jnp.float32), -6.0, 6.0) * scale
    marked = lax.iota(jnp.int32, D) % HD == 0
    return jnp.clip(base + spike * jnp.where(marked[None, :], direction[:, None], 0.0) / math.sqrt(D), -1.0, 1.0)


def draw_source_hidden(key, part):
    key = jax.random.fold_in(key, 31)
    return jnp.clip(jax.random.normal(key, (SRC_LEN, D), jnp.float32), -6.0, 6.0).astype(jnp.bfloat16)


def draw_target_hidden(key, part):
    key = jax.random.fold_in(key, 37)
    return jnp.clip(jax.random.normal(key, (TGT_LEN, D), jnp.float32), -6.0, 6.0).astype(jnp.bfloat16)


def draw_query_weight(key, part):
    direction = shared_direction(key)
    key = jax.random.fold_in(key, 41)
    return weight_matrix(key, 2.0 / math.sqrt(D), 0.0, direction).astype(jnp.bfloat16)


def draw_key_weight(key, part):
    direction = shared_direction(key)
    key = jax.random.fold_in(key, 43)
    return weight_matrix(key, 1.0 / math.sqrt(D), 0.0, direction).astype(jnp.bfloat16)


def draw_cross_query(key, part):
    direction = shared_direction(key)
    key = jax.random.fold_in(key, 47)
    return weight_matrix(key, 2.0 / math.sqrt(D), 0.0, direction).astype(jnp.bfloat16)


def draw_cross_key(key, part):
    direction = shared_direction(key)
    key = jax.random.fold_in(key, 53)
    return weight_matrix(key, 1.0 / math.sqrt(D), 0.0, direction).astype(jnp.bfloat16)


def steps_of(own_key, dims, shards, low, high):
    loudness = 1.0
    for axis_at, blocks in shards:
        steps = jax.random.uniform(jax.random.fold_in(jax.random.fold_in(own_key, 6), axis_at), (blocks,), jnp.float32, low / len(shards), high / len(shards))
        loudness = loudness * jnp.repeat(jnp.exp(steps), dims[axis_at] // blocks).reshape((-1,) + (1,) * (len(dims) - 1 - axis_at))
    return loudness


def scatter_about(own_key, shape, width, most, pieces=(), kind=jnp.bfloat16):
    values = width * jax.random.normal(own_key, shape, jnp.float32)
    if pieces:
        values = values * steps_of(own_key, shape, pieces, -0.22, 0.18)
    return jnp.clip(values, -most, most).astype(kind)


def setup_inputs(seed: int = 0) -> dict:
    streams_of = jax.random.split(jax.random.key(seed), 15)
    source_hidden = draw_source_hidden(jax.random.fold_in(streams_of[14], 71), 0)
    target_hidden = draw_target_hidden(jax.random.fold_in(streams_of[14], 71), 0)
    source_length = jax.random.randint(streams_of[2], (1,), SRC_LEN // 2, SRC_LEN + 1).astype(jnp.int32)
    target_length = jax.random.randint(streams_of[3], (1,), TGT_LEN // 2, TGT_LEN + 1).astype(jnp.int32)
    encoder_gain = jnp.clip(1.0 + 0.15 * jax.random.normal(streams_of[4], (D,), jnp.float32), 0.25, 1.75)
    query_weight = draw_query_weight(jax.random.fold_in(streams_of[14], 71), 0)
    key_weight = draw_key_weight(jax.random.fold_in(streams_of[14], 71), 0)
    value_weight = scatter_about(streams_of[7], (D, D), HD ** -0.5, 0.5, ((1, 16),))
    output_weight = scatter_about(streams_of[8], (D, D), HD ** -0.5, 0.5, ((0, 16),))
    final_gain = jnp.clip(1.0 + 0.15 * jax.random.normal(streams_of[9], (D,), jnp.float32), 0.25, 1.75)
    cross_query = draw_cross_query(jax.random.fold_in(streams_of[14], 71), 0)
    cross_key = draw_cross_key(jax.random.fold_in(streams_of[14], 71), 0)
    cross_value = scatter_about(streams_of[12], (D, D), HD ** -0.5, 0.5, ((1, 16),))
    cross_gain = jnp.clip(1.0 + 0.15 * jax.random.normal(streams_of[13], (D,), jnp.float32), 0.25, 1.75)
    return dict(source_hidden=source_hidden, target_hidden=target_hidden, source_length=source_length, target_length=target_length, encoder_gain=encoder_gain, query_weight=query_weight, key_weight=key_weight, value_weight=value_weight, output_weight=output_weight, final_gain=final_gain, cross_query=cross_query, cross_key=cross_key, cross_value=cross_value, cross_gain=cross_gain)


EPSILON = 1e-05
MASKED = -1e+30

def layer_norm(hidden, scale_gain):
    floats = hidden.astype(jnp.float32)
    center = floats - lax.optimization_barrier(jnp.mean(floats, axis=-1, keepdims=True))
    spread = lax.optimization_barrier(jnp.mean(center * center, axis=-1, keepdims=True))
    return (center * lax.rsqrt(spread + EPSILON) * scale_gain).astype(jnp.bfloat16)

def project(normed, weight):
    return jnp.dot(normed, weight, preferred_element_type=jnp.float32).astype(jnp.bfloat16)

def attend(queries, key_rows, value_rows, usable):
    scores = jnp.dot(queries, key_rows.T, preferred_element_type=jnp.float32) * HD ** (-0.5)
    scores = jnp.where(usable[None, :], scores, MASKED)
    top_score = lax.optimization_barrier(jnp.max(scores, axis=-1, keepdims=True))
    weights = jnp.where(usable[None, :], jnp.exp(scores - top_score), 0.0)
    denominator = lax.optimization_barrier(jnp.sum(weights, axis=-1, keepdims=True))
    context = jnp.dot(weights.astype(jnp.bfloat16), value_rows, preferred_element_type=jnp.float32)
    return context / denominator

def all_heads(queries, key_rows, value_rows, usable):
    row_count = queries.shape[0]
    block_size = math.gcd(row_count, 1024)
    query_heads = queries.reshape(row_count // block_size, block_size, H, HD).transpose(2, 0, 1, 3)
    key_heads = key_rows.reshape(-1, H, HD).transpose(1, 0, 2)
    value_heads = value_rows.reshape(-1, H, HD).transpose(1, 0, 2)

    def per_head(head_item):
        query_blocks, key_one, value_one = head_item

        def per_block(query_block):
            return attend(query_block, key_one, value_one, usable)
        return lax.map(per_block, query_blocks)
    attended = lax.map(per_head, (query_heads, key_heads, value_heads))
    return attended.transpose(1, 2, 0, 3).reshape(row_count, H * HD)

def head_sum(encoder_context, output_weight):
    row_count = encoder_context.shape[0]
    context_heads = encoder_context.reshape(row_count, H, HD).transpose(1, 0, 2)
    weight_heads = output_weight.reshape(H, HD, D)

    def add_head(total, item):
        context_one, weight_one = item
        share = jnp.dot(context_one, weight_one, preferred_element_type=jnp.float32).astype(jnp.bfloat16)
        share = lax.optimization_barrier(share)
        return (total + share.astype(jnp.float32), None)
    total, unused = lax.scan(add_head, jnp.zeros((row_count, D), jnp.float32), (context_heads, weight_heads))
    return total

def reference(source_hidden, target_hidden, source_length, target_length, encoder_gain, query_weight, key_weight, value_weight, output_weight, final_gain, cross_query, cross_key, cross_value, cross_gain):
    usable = jnp.arange(SRC_LEN, dtype=jnp.int32) < source_length[0]
    source_norm = layer_norm(source_hidden, encoder_gain)
    queries = project(source_norm, query_weight)
    key_rows = project(source_norm, key_weight)
    value_rows = project(source_norm, value_weight)
    encoder_context = all_heads(queries, key_rows, value_rows, usable).astype(jnp.bfloat16)
    branch = head_sum(encoder_context, output_weight)
    encoder_out = (source_hidden.astype(jnp.float32) + branch).astype(jnp.bfloat16)
    encoder_final = layer_norm(encoder_out, final_gain)
    memory_keys = project(encoder_final, cross_key)
    memory_values = project(encoder_final, cross_value)
    target_norm = layer_norm(target_hidden, cross_gain)
    target_queries = project(target_norm, cross_query)
    crossed = all_heads(target_queries, memory_keys, memory_values, usable)
    live_rows = jnp.arange(TGT_LEN, dtype=jnp.int32)[:, None] < target_length[0]
    cross_context = jnp.where(live_rows, crossed, 0.0).astype(jnp.bfloat16)
    return (encoder_out, cross_context)
```

```python
import functools
import math

import jax
import jax.numpy as jnp
from jax import lax
from jax.experimental import pallas as pl
from jax.experimental.pallas import tpu as pltpu
from jax.sharding import Mesh, PartitionSpec as P

HD = 128
D = 2048
EPSILON = 1e-05
MASKED = -1e30
SCORE_SCALE = HD ** (-0.5) * math.log2(math.e)
F32 = jnp.float32
BF16 = jnp.bfloat16

AXES = (("zl", 2), ("yh", 4), ("yl", 2), ("c", 2), ("zh", 4), ("x", 4))
SEQ = ("zl", "yh", "yl", "c")
HEAD = ("zh", "x")
QUERY_GROUP = ("zl", "yl", "c")
VMEM = pl.BlockSpec(memory_space=pltpu.VMEM)
SMEM = pl.BlockSpec(memory_space=pltpu.SMEM)
VMEM_LIMIT = 48 * 1024 * 1024


def call(kernel, out_shape, *args, specs, scratch=(), flops=0, transcendentals=0):
    outs = jax.tree.leaves(out_shape)
    size = sum(math.prod(a.shape) * a.dtype.itemsize for a in (*args, *outs))
    return pl.pallas_call(
        kernel,
        out_shape=out_shape,
        in_specs=specs,
        out_specs=jax.tree.map(lambda _: VMEM, out_shape),
        scratch_shapes=scratch,
        compiler_params=pltpu.CompilerParams(vmem_limit_bytes=VMEM_LIMIT),
        cost_estimate=pl.CostEstimate(flops=flops, bytes_accessed=size, transcendentals=transcendentals),
    )(*args)


def shape(*dims, dtype=BF16):
    return jax.ShapeDtypeStruct(dims, dtype)


def normed_rows(pieces, gains):
    total = functools.reduce(jnp.add, pieces)
    mean = jnp.sum(total, axis=-1, keepdims=True) * (1.0 / D)
    centers = [p - mean for p in pieces]
    squares = functools.reduce(jnp.add, [c * c for c in centers])
    spread = jnp.sum(squares, axis=-1, keepdims=True) * (1.0 / D)
    inverse = lax.rsqrt(spread + EPSILON)
    return [(c * inverse * g).astype(BF16) for c, g in zip(centers, gains)]


def norm_gathered(x_ref, gain_ref, norm_ref, step=64):
    rows = x_ref.shape[1]

    def body(i, _):
        r = pl.multiple_of(i * step, step)
        pieces = [x_ref[j, pl.ds(r, step), :].astype(F32) for j in range(16)]
        gains = [gain_ref[:, j * 128 : (j + 1) * 128] for j in range(16)]
        for j, n in enumerate(normed_rows(pieces, gains)):
            norm_ref[pl.ds(r, step), j * 128 : (j + 1) * 128] = n
        return 0

    lax.fori_loop(0, rows // step, body, 0)


def qkv_kernel(x_ref, gain_ref, wq_ref, wk_ref, wv_ref, q_ref, kv_ref, norm_ref):
    norm_gathered(x_ref, gain_ref, norm_ref)
    weights = jnp.concatenate([wq_ref[...], wk_ref[...], wv_ref[...]], axis=1)
    out = jnp.dot(norm_ref[...], weights, preferred_element_type=F32)
    q = (out[:, :128] * SCORE_SCALE).astype(BF16)
    k = out[:, 128:256].astype(BF16)
    v = out[:, 256:].astype(BF16)
    for a in range(q_ref.shape[0]):
        q_ref[a] = q
    for b in range(kv_ref.shape[0]):
        kv_ref[b, 0] = k
        kv_ref[b, 1] = v


def target_kernel(x_ref, gain_ref, wq_ref, q_ref, norm_ref):
    norm_gathered(x_ref, gain_ref, norm_ref)
    out = jnp.dot(norm_ref[...], wq_ref[...], preferred_element_type=F32)
    q_ref[...] = (out * SCORE_SCALE).astype(BF16)


def attend_kernel(part, info_ref, q_ref, kv_ref, out_ref, ka_ref, va_ref, qa_ref):
    members, rows, _ = q_ref.shape
    blocks, pieces, _, n, _ = kv_ref.shape
    base, limit, stride = info_ref[0], info_ref[1], info_ref[2]
    lane = lax.broadcasted_iota(jnp.int32, (n, 128), 1)
    row = lax.broadcasted_iota(jnp.int32, (n, 128), 0)
    for b in range(blocks):
        for t in range(pieces):
            at = (b * pieces + t) * n
            place = base + b * stride + t * n + row
            bias = jnp.where((lane == 0) & (place >= limit), MASKED, 0.0).astype(BF16)
            ka_ref[at : at + n, :128] = kv_ref[b, t, 0]
            ka_ref[at : at + n, 128:] = bias
            va_ref[at : at + n, :128] = kv_ref[b, t, 1]
            va_ref[at : at + n, 128:] = jnp.ones((n, 128), BF16)
    qlane = lax.broadcasted_iota(jnp.int32, (rows, 128), 1)
    qa_ref[:, 128:] = jnp.where(qlane == 0, 1.0, 0.0).astype(BF16)
    group = min(part, 128)
    groups = part // group
    eye = lax.broadcasted_iota(jnp.int32, (group, 128), 0) == lax.broadcasted_iota(jnp.int32, (group, 128), 1)
    block = min(rows, 256)

    def body(a, _):
        for r in range(0, rows, block):
            qa_ref[r : r + block, :128] = q_ref[a, r : r + block, :]
            scores = lax.dot_general(
                qa_ref[r : r + block, :], ka_ref[...], (((1,), (1,)), ((), ())), preferred_element_type=F32
            )
            top = jnp.max(scores, axis=1, keepdims=True)
            weights = jnp.exp2(scores - top).astype(BF16)
            summed = jnp.dot(weights, va_ref[...], preferred_element_type=F32)
            denominator = summed[:, 128:]
            context = (summed[:, :128] / denominator).astype(BF16)
            level = top + jnp.log2(denominator)
            for g in range(block // group):
                at = r + g * group
                p, inside = at // part, at % part
                out_ref[a, p, inside : inside + group, :] = context[g * group : (g + 1) * group]
                line = jnp.sum(jnp.where(eye, level[g * group : (g + 1) * group], 0.0), axis=0, keepdims=True)
                stat_ref_store(out_ref, a, p, part, inside // group, groups, line)
        return 0

    lax.fori_loop(0, members, body, 0)


def stat_ref_store(out_ref, a, p, part, g, groups, line):
    high = line.astype(BF16)
    rest = line - high.astype(F32)
    middle = rest.astype(BF16)
    low = (rest - middle.astype(F32)).astype(BF16)
    out_ref[a, p, part + g : part + g + 1, :] = high
    out_ref[a, p, part + groups + g : part + groups + g + 1, :] = middle
    out_ref[a, p, part + 2 * groups + g : part + 2 * groups + g + 1, :] = low


def mixing(levels):
    top = functools.reduce(jnp.maximum, levels)
    raw = [jnp.exp2(v - top) for v in levels]
    total = functools.reduce(jnp.add, raw)
    return [v / total for v in raw]


def combined(read_rows, read_stats, members, part):
    group = min(part, 128)
    groups = part // group
    eye = lax.broadcasted_iota(jnp.int32, (group, 128), 0) == lax.broadcasted_iota(jnp.int32, (group, 128), 1)
    levels = []
    for a in range(members):
        stats = read_stats(a).astype(F32)
        levels.append(stats[:groups] + stats[groups : 2 * groups] + stats[2 * groups : 3 * groups])
    shares = mixing(levels)
    out = []
    for g in range(groups):
        total = None
        for a in range(members):
            column = jnp.sum(jnp.where(eye, shares[a][g : g + 1], 0.0), axis=1, keepdims=True)
            term = read_rows(a)[g * group : (g + 1) * group].astype(F32) * column
            total = term if total is None else total + term
        out.append(total)
    return out


def project_out_kernel(r_ref, w_ref, out_ref, ctx_ref):
    members, heads, full, _ = r_ref.shape
    part = full - 16
    for h in range(heads):
        pieces = combined(
            lambda a: r_ref[a, h, :part, :], lambda a: r_ref[a, h, part:, :], members, part
        )
        ctx_ref[:, h * 128 : (h + 1) * 128] = pieces[0].astype(BF16)
    out = jnp.dot(ctx_ref[...], w_ref[...], preferred_element_type=F32).astype(BF16)
    for z in range(4):
        out_ref[z] = out[z * 16 : (z + 1) * 16]


def residual_kernel(r_ref, s_ref, out_ref):
    for j in range(16):
        cols = slice(j * 128, (j + 1) * 128)
        total = s_ref[j].astype(F32)
        for z in range(4):
            total = total + r_ref[z, :, cols].astype(F32)
        total = total.astype(BF16)
        for z in range(4):
            out_ref[z, :, cols] = total


def memory_kernel(e_ref, gain_ref, wk_ref, wv_ref, kv_ref, norm_ref):
    pieces = [e_ref[:, j * 128 : (j + 1) * 128].astype(F32) for j in range(16)]
    gains = [gain_ref[:, j * 128 : (j + 1) * 128] for j in range(16)]
    for j, n in enumerate(normed_rows(pieces, gains)):
        norm_ref[:, j * 128 : (j + 1) * 128] = n
    for h in range(4):
        weights = jnp.concatenate([wk_ref[h], wv_ref[h]], axis=1)
        out = jnp.dot(norm_ref[...], weights, preferred_element_type=F32).astype(BF16)
        for b in range(4):
            kv_ref[b, h, 0] = out[:, :128]
            kv_ref[b, h, 1] = out[:, 128:]


def finish_kernel(info_ref, r_ref, out_ref):
    members, full, _ = r_ref.shape
    part = full - 16
    pieces = combined(lambda a: r_ref[a, :part, :], lambda a: r_ref[a, part:, :], members, part)
    first, limit = info_ref[0], info_ref[1]
    for g, piece in enumerate(pieces):
        n = piece.shape[0]
        place = first + g * n + lax.broadcasted_iota(jnp.int32, (n, 128), 0)
        out_ref[g * n : (g + 1) * n, :] = jnp.where(place < limit, piece, 0.0).astype(BF16)


def exchange(x, axes):
    return lax.all_to_all(x, axes, 0, 0, tiled=True)


def attend(q, kv, info, part):
    members, rows, _ = q.shape
    keys = kv.shape[0] * kv.shape[1] * kv.shape[3]
    return call(
        functools.partial(attend_kernel, part),
        shape(members, rows // part, part + 16, 128),
        info,
        q,
        kv,
        specs=[SMEM, VMEM, VMEM],
        scratch=[pltpu.VMEM((keys, 256), BF16), pltpu.VMEM((keys, 256), BF16), pltpu.VMEM((rows, 256), BF16)],
        flops=4 * members * rows * keys * 256,
        transcendentals=members * rows * keys,
    )


def shards(
    source_hidden,
    target_hidden,
    source_length,
    target_length,
    encoder_gain,
    query_weight,
    key_weight,
    value_weight,
    output_weight,
    final_gain,
    cross_query,
    cross_key,
    cross_value,
    cross_gain,
):
    rows = source_hidden.shape[0]
    target_rows = target_hidden.shape[0]
    at = {name: lax.axis_index(name) for name, _ in AXES}
    seq_at = ((at["zl"] * 4 + at["yh"]) * 2 + at["yl"]) * 2 + at["c"]
    key_base = ((at["zl"] * 8 + at["yl"]) * 2 + at["c"]) * rows
    key_info = jnp.stack([key_base, source_length[0], jnp.int32(4 * rows)])
    target_info = jnp.stack([seq_at * target_rows, target_length[0]])
    gains = [g.reshape(1, D) for g in (encoder_gain, final_gain, cross_gain)]

    out_weight = lax.all_gather(output_weight, "x", axis=0, tiled=True)
    memory_key_weight = lax.all_gather(cross_key, "x", axis=0)
    memory_value_weight = lax.all_gather(cross_value, "x", axis=0)
    target_full = lax.all_gather(target_hidden, HEAD, axis=0)

    source_full = exchange(jnp.broadcast_to(source_hidden[None], (16, rows, 128)), HEAD)
    queries, keys_values = call(
        qkv_kernel,
        (shape(8, rows, 128), shape(4, 2, rows, 128)),
        source_full,
        gains[0],
        query_weight,
        key_weight,
        value_weight,
        specs=[VMEM] * 5,
        scratch=[pltpu.VMEM((rows, D), BF16)],
        flops=2 * rows * D * 384,
    )
    queries = exchange(queries, QUERY_GROUP)
    keys_values = exchange(keys_values, "yh")
    partial = attend(queries, keys_values.reshape(4, 1, 2, rows, 128), key_info, rows // 4)
    partial = exchange(partial.reshape(32, rows // 4 + 16, 128), QUERY_GROUP + ("x",))
    quarter = rows // 4
    shares = call(
        project_out_kernel,
        shape(4, quarter // 4, D),
        partial.reshape(8, 4, quarter + 16, 128),
        out_weight,
        specs=[VMEM] * 2,
        scratch=[pltpu.VMEM((quarter, 512), BF16)],
        flops=2 * quarter * 512 * D,
    )
    shares = exchange(shares, "zh")
    first = at["x"] * quarter + at["zh"] * (quarter // 4)
    own_source = lax.dynamic_slice_in_dim(source_full, first, quarter // 4, 1)
    encoder_rows = call(
        residual_kernel, shape(4, quarter // 4, D), shares, own_source, specs=[VMEM] * 2
    )
    encoder_rows = exchange(encoder_rows, "zh").reshape(quarter, D)
    memory = call(
        memory_kernel,
        shape(4, 4, 2, quarter, 128),
        encoder_rows,
        gains[1],
        memory_key_weight,
        memory_value_weight,
        specs=[VMEM] * 4,
        scratch=[pltpu.VMEM((quarter, D), BF16)],
        flops=2 * quarter * D * 1024,
    )
    encoder_full = lax.all_gather(encoder_rows, "x", axis=0, tiled=True)
    head_at = at["zh"] * 4 + at["x"]
    encoder_out = lax.dynamic_slice_in_dim(encoder_full, head_at * 128, 128, 1)

    target_queries = call(
        target_kernel,
        shape(target_rows, 128),
        target_full,
        gains[2],
        cross_query,
        specs=[VMEM] * 3,
        scratch=[pltpu.VMEM((target_rows, D), BF16)],
        flops=2 * target_rows * D * 128,
    )
    target_queries = lax.all_gather(target_queries, QUERY_GROUP, axis=0)
    memory = exchange(memory.reshape(16, 2, quarter, 128), ("yh", "x")).reshape(4, 4, 2, quarter, 128)
    crossed = attend(target_queries, memory, key_info, target_rows)
    crossed = exchange(crossed.reshape(8, target_rows + 16, 128), QUERY_GROUP)
    cross_context = call(
        finish_kernel, shape(target_rows, 128), target_info, crossed, specs=[SMEM, VMEM]
    )
    return (encoder_out, cross_context)


def solution(mesh):
    fine = Mesh(mesh.devices.reshape([size for _, size in AXES]), [name for name, _ in AXES])
    columns = P(None, HEAD)
    in_specs = (
        P(SEQ, HEAD),
        P(SEQ, HEAD),
        P(),
        P(),
        P(),
        columns,
        columns,
        columns,
        P(HEAD, None),
        P(),
        columns,
        columns,
        columns,
        P(),
    )
    out_specs = (P(SEQ, HEAD), P(SEQ, HEAD))
    return jax.shard_map(shards, mesh=fine, in_specs=in_specs, out_specs=out_specs, check_vma=False)
```

```python
import functools
import math

import jax
import jax.numpy as jnp
from jax import lax
from jax.experimental import pallas as pl
from jax.experimental.pallas import tpu as pltpu
from jax.sharding import Mesh, PartitionSpec as P

HD = 128
D = 2048
EPSILON = 1e-05
MASKED = -1e30
SCORE_SCALE = HD ** (-0.5) * math.log2(math.e)
F32 = jnp.float32
BF16 = jnp.bfloat16

AXES = (("zl", 2), ("yh", 4), ("yl", 2), ("c", 2), ("zh", 4), ("x", 4))
SEQ = ("zl", "yh", "yl", "c")
HEAD = ("zh", "x")
QUERY_GROUP = ("zl", "yl", "c")
VMEM = pl.BlockSpec(memory_space=pltpu.VMEM)
SMEM = pl.BlockSpec(memory_space=pltpu.SMEM)
ANY = pl.BlockSpec(memory_space=pl.ANY)
HBM = pl.BlockSpec(memory_space=pltpu.HBM)
DMA = pltpu.SemaphoreType.DMA


def call(kernel, out_shape, *args, specs, out=None, scratch=(), limit=48, flops=0, transcendentals=0):
    outs = jax.tree.leaves(out_shape)
    size = sum(math.prod(a.shape) * a.dtype.itemsize for a in (*args, *outs))
    return pl.pallas_call(
        kernel,
        out_shape=out_shape,
        in_specs=specs,
        out_specs=jax.tree.map(lambda _: VMEM, out_shape) if out is None else out,
        scratch_shapes=scratch,
        compiler_params=pltpu.CompilerParams(vmem_limit_bytes=int(limit * 1024 * 1024)),
        cost_estimate=pl.CostEstimate(flops=flops, bytes_accessed=size, transcendentals=transcendentals),
    )(*args)


def shape(*dims, dtype=BF16):
    return jax.ShapeDtypeStruct(dims, dtype)


def started(pairs, sems):
    copies = [pltpu.make_async_copy(a, b, sems.at[i]) for i, (a, b) in enumerate(pairs)]
    for copy in copies:
        copy.start()
    return copies


def wait_for(copies):
    for copy in copies:
        copy.wait()


def repeat_kernel(x_ref, out_ref, sems):
    wait_for(started([(x_ref, out_ref.at[i]) for i in range(out_ref.shape[0])], sems))


def repeated(x, times):
    return call(
        repeat_kernel, shape(times, *x.shape), x, specs=[VMEM], out=HBM, scratch=[DMA((times,))], limit=63.9
    )


def normed_rows(pieces, gains):
    total = functools.reduce(jnp.add, pieces)
    mean = jnp.sum(total, axis=-1, keepdims=True) * (1.0 / D)
    centers = [p - mean for p in pieces]
    squares = functools.reduce(jnp.add, [c * c for c in centers])
    spread = jnp.sum(squares, axis=-1, keepdims=True) * (1.0 / D)
    inverse = lax.rsqrt(spread + EPSILON)
    return [(c * inverse * g).astype(BF16) for c, g in zip(centers, gains)]


def norm_gathered(x_ref, gain_ref, norm_ref, step=64):
    rows = x_ref.shape[1]

    def body(i, _):
        r = pl.multiple_of(i * step, step)
        pieces = [x_ref[j, pl.ds(r, step), :].astype(F32) for j in range(16)]
        gains = [gain_ref[:, j * 128 : (j + 1) * 128] for j in range(16)]
        for j, n in enumerate(normed_rows(pieces, gains)):
            norm_ref[pl.ds(r, step), j * 128 : (j + 1) * 128] = n
        return 0

    lax.fori_loop(0, rows // step, body, 0)


def qkv_kernel(x_ref, gain_ref, wq_ref, wk_ref, wv_ref, q_ref, kv_ref, norm_ref, w_ref, q_one_ref, in_sems, out_sems):
    weights = started(
        [(w, w_ref.at[:, i * 128 : (i + 1) * 128]) for i, w in enumerate((wq_ref, wk_ref, wv_ref))], in_sems
    )
    norm_gathered(x_ref, gain_ref, norm_ref)
    wait_for(weights)
    out = jnp.dot(norm_ref[...], w_ref[...], preferred_element_type=F32)
    q_one_ref[...] = (out[:, :128] * SCORE_SCALE).astype(BF16)
    copies = started([(q_one_ref, q_ref.at[a]) for a in range(q_ref.shape[0])], out_sems)
    kv_ref[0] = out[:, 128:256].astype(BF16)
    kv_ref[1] = out[:, 256:].astype(BF16)
    wait_for(copies)


def target_kernel(x_ref, gain_ref, wq_ref, q_ref, norm_ref, x_vmem, w_ref, x_sems, w_sem):
    rows = x_ref.shape[1]
    parts = x_vmem.shape[0]
    step = rows // parts
    weights = started([(wq_ref, w_ref)], w_sem)
    pieces = started(
        [(x_ref.at[:, i * step : (i + 1) * step, :], x_vmem.at[i]) for i in range(parts)], x_sems
    )
    for i, piece in enumerate(pieces):
        piece.wait()
        norm_gathered(x_vmem.at[i], gain_ref, norm_ref.at[i * step : (i + 1) * step, :])
    wait_for(weights)
    out = jnp.dot(norm_ref[...], w_ref[...], preferred_element_type=F32)
    q_ref[...] = (out * SCORE_SCALE).astype(BF16)


def attend_kernel(part, blocks, fetched, info_ref, q_ref, *refs):
    kv_refs, (out_ref, ka_ref, va_ref, *q_scratch) = refs[: len(refs) - 3 - fetched * 2], refs[len(refs) - 3 - fetched * 2 :]
    members, rows, _ = q_ref.shape
    q_vmem, q_copy = q_ref, []
    if fetched:
        q_vmem, q_sem = q_scratch
        q_copy = started([(q_ref, q_vmem)], q_sem)
    limit = info_ref[0]
    n = kv_refs[0].shape[-2]
    lane = lax.broadcasted_iota(jnp.int32, (n, 128), 1)
    row = lax.broadcasted_iota(jnp.int32, (n, 128), 0)
    for b, (ref, at) in enumerate(blocks):
        place = info_ref[1 + b] + row
        bias = jnp.where((lane == 0) & (place >= limit), MASKED, 0.0).astype(BF16)
        here = slice(b * n, (b + 1) * n)
        ka_ref[here, :128] = kv_refs[ref][(*at, 0)]
        ka_ref[here, 128:] = bias
        va_ref[here, :128] = kv_refs[ref][(*at, 1)]
        va_ref[here, 128:] = jnp.ones((n, 128), BF16)
    ones = jnp.where(lax.broadcasted_iota(jnp.int32, (256, 128), 1) == 0, 1.0, 0.0).astype(BF16)
    group = min(part, 128)
    groups = part // group
    eye = lax.broadcasted_iota(jnp.int32, (group, 128), 0) == lax.broadcasted_iota(jnp.int32, (group, 128), 1)
    block = 256
    each = rows // block
    unroll = 8

    wait_for(q_copy)

    def body(i, _):
        for u in range(unroll):
            step = i * unroll + u
            a, r = (step, 0) if each == 1 else (step // each, (u % each) * block)
            q = jnp.concatenate([q_vmem[a, pl.ds(r, block), :], ones], axis=1)
            scores = lax.dot_general(q, ka_ref[...], (((1,), (1,)), ((), ())), preferred_element_type=F32)
            top = jnp.max(scores, axis=1, keepdims=True)
            weights = jnp.exp2(scores - top).astype(BF16)
            summed = jnp.dot(weights, va_ref[...], preferred_element_type=F32)
            denominator = summed[:, 128:]
            context = (summed[:, :128] / denominator).astype(BF16)
            level = top + jnp.log2(denominator)
            for g in range(block // group):
                at = r + g * group
                p, inside = at // part, at % part
                out_ref[a, p, inside : inside + group, :] = context[g * group : (g + 1) * group]
                line = jnp.sum(jnp.where(eye, level[g * group : (g + 1) * group], 0.0), axis=0, keepdims=True)
                stat_ref_store(out_ref, a, p, part, inside // group, groups, line)
        return 0

    lax.fori_loop(0, members * each // unroll, body, 0)


def stat_ref_store(out_ref, a, p, part, g, groups, line):
    high = line.astype(BF16)
    rest = line - high.astype(F32)
    middle = rest.astype(BF16)
    low = (rest - middle.astype(F32)).astype(BF16)
    out_ref[a, p, part + g : part + g + 1, :] = high
    out_ref[a, p, part + groups + g : part + groups + g + 1, :] = middle
    out_ref[a, p, part + 2 * groups + g : part + 2 * groups + g + 1, :] = low


def mixing(levels):
    top = functools.reduce(jnp.maximum, levels)
    raw = [jnp.exp2(v - top) for v in levels]
    total = functools.reduce(jnp.add, raw)
    return [v / total for v in raw]


def combined(read_rows, read_stats, members, part):
    group = min(part, 128)
    groups = part // group
    eye = lax.broadcasted_iota(jnp.int32, (group, 128), 0) == lax.broadcasted_iota(jnp.int32, (group, 128), 1)
    levels = []
    for a in range(members):
        stats = read_stats(a).astype(F32)
        levels.append(stats[:groups] + stats[groups : 2 * groups] + stats[2 * groups : 3 * groups])
    shares = mixing(levels)
    out = []
    for g in range(groups):
        total = None
        for a in range(members):
            column = jnp.sum(jnp.where(eye, shares[a][g : g + 1], 0.0), axis=1, keepdims=True)
            term = read_rows(a)[g * group : (g + 1) * group].astype(F32) * column
            total = term if total is None else total + term
        out.append(total)
    return out


def project_out_kernel(info_ref, r_ref, own_ref, mine_ref, theirs_ref, out_ref, ctx_ref, w_ref, sems):
    core = info_ref[0]
    half = D // 2
    copies = started(
        [(own_ref, w_ref.at[:128])]
        + [
            (ref.at[k], w_ref.at[(k + 1) * 128 : (k + 2) * 128, pl.ds(pl.multiple_of(first * half, half), half)])
            for ref, first in ((mine_ref, core), (theirs_ref, 1 - core))
            for k in range(3)
        ],
        sems,
    )
    members, _, full, _ = r_ref.shape
    part = full - 16
    for k in range(4):
        h = info_ref[1 + k]
        pieces = combined(
            lambda a: r_ref[a, h, :part, :], lambda a: r_ref[a, h, part:, :], members, part
        )
        ctx_ref[:, k * 128 : (k + 1) * 128] = pieces[0].astype(BF16)
    wait_for(copies)
    out = jnp.dot(ctx_ref[...], w_ref[...], preferred_element_type=F32).astype(BF16)
    for z in range(4):
        out_ref[z] = out[z * 16 : (z + 1) * 16]


def residual_kernel(r_ref, s_ref, out_ref):
    for j in range(16):
        cols = slice(j * 128, (j + 1) * 128)
        total = s_ref[j].astype(F32)
        for z in range(4):
            total = total + r_ref[z, :, cols].astype(F32)
        total = total.astype(BF16)
        for z in range(4):
            out_ref[z, :, cols] = total


def memory_kernel(info_ref, e_ref, gain_ref, mine_ref, theirs_ref, kv_ref, norm_ref, e_vmem, w_ref, sems, e_sem):
    core = info_ref[0]
    half = D // 2
    rows = started([(e_ref, e_vmem)], e_sem)
    copies = started(
        [
            (ref.at[h, t], w_ref.at[h, pl.ds(pl.multiple_of(first * half, half), half), t * 128 : (t + 1) * 128])
            for h in range(4)
            for ref, first in ((mine_ref, core), (theirs_ref, 1 - core))
            for t in range(2)
        ],
        sems,
    )
    wait_for(rows)
    pieces = [e_vmem[:, j * 128 : (j + 1) * 128].astype(F32) for j in range(16)]
    gains = [gain_ref[:, j * 128 : (j + 1) * 128] for j in range(16)]
    for j, n in enumerate(normed_rows(pieces, gains)):
        norm_ref[:, j * 128 : (j + 1) * 128] = n
    for h in range(4):
        wait_for(copies[h * 4 : (h + 1) * 4])
        out = jnp.dot(norm_ref[...], w_ref[h], preferred_element_type=F32).astype(BF16)
        for b in range(4):
            kv_ref[b, h, 0] = out[:, :128]
            kv_ref[b, h, 1] = out[:, 128:]


def finish_kernel(info_ref, r_ref, out_ref):
    members, full, _ = r_ref.shape
    part = full - 16
    pieces = combined(lambda a: r_ref[a, :part, :], lambda a: r_ref[a, part:, :], members, part)
    first, limit = info_ref[0], info_ref[1]
    for g, piece in enumerate(pieces):
        n = piece.shape[0]
        place = first + g * n + lax.broadcasted_iota(jnp.int32, (n, 128), 0)
        out_ref[g * n : (g + 1) * n, :] = jnp.where(place < limit, piece, 0.0).astype(BF16)


def exchange(x, axes):
    return lax.all_to_all(x, axes, 0, 0, tiled=True)


def attend(q, kvs, blocks, info, part, fetched):
    members, rows, _ = q.shape
    keys = len(blocks) * kvs[0].shape[-2]
    return call(
        functools.partial(attend_kernel, part, blocks, fetched),
        shape(members, rows // part, part + 16, 128),
        info,
        q,
        *kvs,
        specs=[SMEM, ANY if fetched else VMEM] + [VMEM] * len(kvs),
        scratch=[pltpu.VMEM((keys, 256), BF16), pltpu.VMEM((keys, 256), BF16)]
        + ([pltpu.VMEM(q.shape, BF16), DMA((1,))] if fetched else []),
        limit=62 if fetched else 48,
        flops=4 * members * rows * keys * 256,
        transcendentals=members * rows * keys,
    )


def swapped(x, axis, size, by):
    return lax.ppermute(x, axis, [(i, i ^ by) for i in range(size)])


def together(*arrays):
    return lax.optimization_barrier(arrays)


def shards(
    source_hidden,
    target_hidden,
    source_length,
    target_length,
    encoder_gain,
    query_weight,
    key_weight,
    value_weight,
    output_weight,
    final_gain,
    cross_query,
    cross_key,
    cross_value,
    cross_gain,
):
    rows = source_hidden.shape[0]
    target_rows = target_hidden.shape[0]
    at = {name: lax.axis_index(name) for name, _ in AXES}
    seq_at = ((at["zl"] * 4 + at["yh"]) * 2 + at["yl"]) * 2 + at["c"]
    quarter = rows // 4
    core_info = jnp.stack([at["c"], at["x"], at["x"] ^ 1, at["x"] ^ 3, at["x"] ^ 2])

    def first_of(yh):
        return (((at["zl"] * 4 + yh) * 2 + at["yl"]) * 2 + at["c"]) * rows

    key_info = jnp.stack([source_length[0]] + [first_of(at["yh"] ^ k) for k in range(4)])
    memory_info = jnp.stack(
        [source_length[0]] + [first_of(k // 4) + (k % 4) * quarter for k in range(16)]
    )
    target_info = jnp.stack([seq_at * target_rows, target_length[0]])
    gains = [g.reshape(1, D) for g in (encoder_gain, final_gain, cross_gain)]

    half = at["c"] * (D // 2)
    out_half = lax.dynamic_slice_in_dim(output_weight, half, D // 2, 1)
    out_halves = [swapped(out_half, "x", 4, k) for k in (1, 3)]
    target_full = lax.all_gather(target_hidden, HEAD, axis=0)
    source_full = exchange(repeated(source_hidden, 16), HEAD)
    source_full, *out_halves = together(source_full, *out_halves)
    out_halves.append(swapped(out_halves[0], "x", 4, 3))
    half_weights = jnp.stack([lax.dynamic_slice_in_dim(w, half, D // 2, 0) for w in (cross_key, cross_value)])
    source_full, half_weights = together(source_full, half_weights)
    mine = lax.all_gather(half_weights, "x", axis=0)

    queries, keys_values = call(
        qkv_kernel,
        (shape(8, rows, 128), shape(2, rows, 128)),
        source_full,
        gains[0],
        query_weight,
        key_weight,
        value_weight,
        specs=[VMEM, VMEM, ANY, ANY, ANY],
        out=(HBM, VMEM),
        scratch=[
            pltpu.VMEM((rows, D), BF16),
            pltpu.VMEM((D, 384), BF16),
            pltpu.VMEM((rows, 128), BF16),
            DMA((3,)),
            DMA((8,)),
        ],
        flops=2 * rows * D * 384,
    )
    key_sets = [keys_values] + [swapped(keys_values, "yh", 4, k) for k in (1, 2, 3)]
    queries = exchange(queries, QUERY_GROUP)
    queries, out_halves[2] = together(queries, out_halves[2])
    out_mine = jnp.stack(out_halves)
    out_theirs = swapped(out_mine, "c", 2, 1)
    partial = attend(queries, key_sets, [(k, ()) for k in range(4)], key_info, quarter, False)
    partial = exchange(partial.reshape(32, rows // 4 + 16, 128), QUERY_GROUP + ("x",))
    target_queries = call(
        target_kernel,
        shape(target_rows, 128),
        target_full,
        gains[2],
        cross_query,
        specs=[ANY, VMEM, ANY],
        scratch=[
            pltpu.VMEM((target_rows, D), BF16),
            pltpu.VMEM((4, 16, target_rows // 4, 128), BF16),
            pltpu.VMEM((D, 128), BF16),
            DMA((4,)),
            DMA((1,)),
        ],
        flops=2 * target_rows * D * 128,
    )
    partial, target_queries = together(partial, target_queries)
    shares = call(
        project_out_kernel,
        shape(4, quarter // 4, D),
        core_info,
        partial.reshape(8, 4, quarter + 16, 128),
        output_weight,
        out_mine,
        out_theirs,
        specs=[SMEM, VMEM] + [ANY] * 3,
        scratch=[pltpu.VMEM((quarter, 512), BF16), pltpu.VMEM((512, D), BF16), DMA((7,))],
        limit=62.5,
        flops=2 * quarter * 512 * D,
    )
    shares = exchange(shares, "zh")
    shares, mine = together(shares, mine)
    theirs = swapped(mine, "c", 2, 1)
    first = at["x"] * quarter + at["zh"] * (quarter // 4)
    own_source = lax.dynamic_slice_in_dim(source_full, first, quarter // 4, 1)
    encoder_rows = call(
        residual_kernel, shape(4, quarter // 4, D), shares, own_source, specs=[VMEM] * 2
    )
    encoder_rows = exchange(encoder_rows, "zh").reshape(quarter, D)
    memory = call(
        memory_kernel,
        shape(4, 4, 2, quarter, 128),
        core_info,
        encoder_rows,
        gains[1],
        mine,
        theirs,
        specs=[SMEM, ANY, VMEM, ANY, ANY],
        scratch=[
            pltpu.VMEM((quarter, D), BF16),
            pltpu.VMEM((quarter, D), BF16),
            pltpu.VMEM((4, D, 256), BF16),
            DMA((16,)),
            DMA((1,)),
        ],
        limit=63,
        flops=2 * quarter * D * 1024,
    )
    encoder_full = lax.all_gather(encoder_rows, "x", axis=0, tiled=True)

    target_queries = lax.all_gather(target_queries, QUERY_GROUP, axis=0)
    memory = exchange(memory.reshape(16, 2, quarter, 128), ("yh", "x")).reshape(4, 4, 2, quarter, 128)
    crossed = attend(
        target_queries, [memory], [(0, (k // 4, k % 4)) for k in range(16)], memory_info, target_rows, True
    )
    crossed, encoder_full = together(crossed, encoder_full)
    crossed = exchange(crossed.reshape(8, target_rows + 16, 128), QUERY_GROUP)
    head_at = at["zh"] * 4 + at["x"]
    encoder_out = lax.dynamic_slice_in_dim(encoder_full, head_at * 128, 128, 1)
    cross_context = call(
        finish_kernel, shape(target_rows, 128), target_info, crossed, specs=[SMEM, VMEM]
    )
    return (encoder_out, cross_context)


def solution(mesh):
    fine = Mesh(mesh.devices.reshape([size for _, size in AXES]), [name for name, _ in AXES])
    columns = P(None, HEAD)
    in_specs = (
        P(SEQ, HEAD),
        P(SEQ, HEAD),
        P(),
        P(),
        P(),
        columns,
        columns,
        columns,
        P(HEAD, None),
        P(),
        columns,
        columns,
        columns,
        P(),
    )
    out_specs = (P(SEQ, HEAD), P(SEQ, HEAD))
    return jax.shard_map(shards, mesh=fine, in_specs=in_specs, out_specs=out_specs, check_vma=False)
```

```python
import functools
import math

import jax
import jax.numpy as jnp
from jax import lax
from jax.experimental import pallas as pl
from jax.experimental.pallas import tpu as pltpu
from jax.sharding import Mesh, PartitionSpec as P

HD = 128
D = 2048
EPSILON = 1e-05
MASKED = -1e30
SCORE_SCALE = HD ** (-0.5) * math.log2(math.e)
F32 = jnp.float32
BF16 = jnp.bfloat16

AXES = (("zl", 2), ("yh", 4), ("yl", 2), ("c", 2), ("zh", 4), ("x", 4))
SEQ = ("zl", "yh", "yl", "c")
HEAD = ("zh", "x")
QUERY_GROUP = ("zl", "yl", "c")
VMEM = pl.BlockSpec(memory_space=pltpu.VMEM)
SMEM = pl.BlockSpec(memory_space=pltpu.SMEM)
ANY = pl.BlockSpec(memory_space=pl.ANY)
HBM = pl.BlockSpec(memory_space=pltpu.HBM)
DMA = pltpu.SemaphoreType.DMA


def call(kernel, out_shape, *args, specs, out=None, scratch=(), limit=48, flops=0, transcendentals=0):
    outs = jax.tree.leaves(out_shape)
    size = sum(math.prod(a.shape) * a.dtype.itemsize for a in (*args, *outs))
    return pl.pallas_call(
        kernel,
        out_shape=out_shape,
        in_specs=specs,
        out_specs=jax.tree.map(lambda _: VMEM, out_shape) if out is None else out,
        scratch_shapes=scratch,
        compiler_params=pltpu.CompilerParams(vmem_limit_bytes=int(limit * 1024 * 1024)),
        cost_estimate=pl.CostEstimate(flops=flops, bytes_accessed=size, transcendentals=transcendentals),
    )(*args)


def shape(*dims, dtype=BF16):
    return jax.ShapeDtypeStruct(dims, dtype)


def started(pairs, sems):
    copies = [pltpu.make_async_copy(a, b, sems.at[i]) for i, (a, b) in enumerate(pairs)]
    for copy in copies:
        copy.start()
    return copies


def wait_for(copies):
    for copy in copies:
        copy.wait()


def repeat_kernel(x_ref, out_ref, sems):
    wait_for(started([(x_ref, out_ref.at[i]) for i in range(out_ref.shape[0])], sems))


def repeated(x, times, limit):
    return call(
        repeat_kernel, shape(times, *x.shape), x, specs=[VMEM], out=HBM, scratch=[DMA((times,))], limit=limit
    )


def normed_rows(pieces, gains):
    total = functools.reduce(jnp.add, pieces)
    mean = jnp.sum(total, axis=-1, keepdims=True) * (1.0 / D)
    centers = [p - mean for p in pieces]
    squares = functools.reduce(jnp.add, [c * c for c in centers])
    spread = jnp.sum(squares, axis=-1, keepdims=True) * (1.0 / D)
    inverse = lax.rsqrt(spread + EPSILON)
    return [(c * inverse * g).astype(BF16) for c, g in zip(centers, gains)]


def x_first(j):
    return (j % 4) * 4 + j // 4


def norm_gathered(x_ref, gain_ref, norm_ref, order=lambda j: j, step=64):
    rows = x_ref.shape[1]

    def body(i, _):
        r = pl.multiple_of(i * step, step)
        pieces = [x_ref[order(j), pl.ds(r, step), :].astype(F32) for j in range(16)]
        gains = [gain_ref[:, j * 128 : (j + 1) * 128] for j in range(16)]
        for j, n in enumerate(normed_rows(pieces, gains)):
            norm_ref[pl.ds(r, step), j * 128 : (j + 1) * 128] = n
        return 0

    lax.fori_loop(0, rows // step, body, 0)


def qkv_kernel(x_ref, gain_ref, wq_ref, wk_ref, wv_ref, q_ref, kv_ref, norm_ref, w_ref, q_one_ref, in_sems, out_sems):
    weights = started(
        [(w, w_ref.at[:, i * 128 : (i + 1) * 128]) for i, w in enumerate((wq_ref, wk_ref, wv_ref))], in_sems
    )
    norm_gathered(x_ref, gain_ref, norm_ref, x_first)
    wait_for(weights)
    out = jnp.dot(norm_ref[...], w_ref[...], preferred_element_type=F32)
    q_one_ref[...] = (out[:, :128] * SCORE_SCALE).astype(BF16)
    copies = started([(q_one_ref, q_ref.at[a]) for a in range(q_ref.shape[0])], out_sems)
    kv_ref[0] = out[:, 128:256].astype(BF16)
    kv_ref[1] = out[:, 256:].astype(BF16)
    wait_for(copies)


def target_kernel(x_ref, gain_ref, wq_ref, q_ref, norm_ref, x_vmem, w_ref, x_sems, w_sem):
    rows = x_ref.shape[1]
    parts = x_vmem.shape[0]
    step = rows // parts
    weights = started([(wq_ref, w_ref)], w_sem)
    pieces = started(
        [(x_ref.at[:, i * step : (i + 1) * step, :], x_vmem.at[i]) for i in range(parts)], x_sems
    )
    for i, piece in enumerate(pieces):
        piece.wait()
        norm_gathered(x_vmem.at[i], gain_ref, norm_ref.at[i * step : (i + 1) * step, :])
    wait_for(weights)
    out = jnp.dot(norm_ref[...], w_ref[...], preferred_element_type=F32)
    q_ref[...] = (out * SCORE_SCALE).astype(BF16)


def attend_kernel(part, blocks, fetched, info_ref, q_ref, *refs):
    kv_refs, (out_ref, ka_ref, va_ref, *q_scratch) = refs[: len(refs) - 3 - fetched * 2], refs[len(refs) - 3 - fetched * 2 :]
    members, rows, _ = q_ref.shape
    q_vmem, q_copy = q_ref, []
    if fetched:
        q_vmem, q_sem = q_scratch
        q_copy = started([(q_ref, q_vmem)], q_sem)
    limit = info_ref[0]
    n = kv_refs[0].shape[-2]
    lane = lax.broadcasted_iota(jnp.int32, (n, 128), 1)
    row = lax.broadcasted_iota(jnp.int32, (n, 128), 0)
    for b, (ref, at) in enumerate(blocks):
        place = info_ref[1 + b] + row
        bias = jnp.where((lane == 0) & (place >= limit), MASKED, 0.0).astype(BF16)
        here = slice(b * n, (b + 1) * n)
        ka_ref[here, :128] = kv_refs[ref][(*at, 0)]
        ka_ref[here, 128:] = bias
        va_ref[here, :128] = kv_refs[ref][(*at, 1)]
        va_ref[here, 128:] = jnp.ones((n, 128), BF16)
    ones = jnp.where(lax.broadcasted_iota(jnp.int32, (256, 128), 1) == 0, 1.0, 0.0).astype(BF16)
    group = min(part, 128)
    groups = part // group
    eye = lax.broadcasted_iota(jnp.int32, (group, 128), 0) == lax.broadcasted_iota(jnp.int32, (group, 128), 1)
    block = 256
    each = rows // block
    unroll = 8

    wait_for(q_copy)

    def body(i, _):
        for u in range(unroll):
            step = i * unroll + u
            a, r = (step, 0) if each == 1 else (step // each, (u % each) * block)
            q = jnp.concatenate([q_vmem[a, pl.ds(r, block), :], ones], axis=1)
            scores = lax.dot_general(q, ka_ref[...], (((1,), (1,)), ((), ())), preferred_element_type=F32)
            top = jnp.max(scores, axis=1, keepdims=True)
            weights = jnp.exp2(scores - top).astype(BF16)
            summed = jnp.dot(weights, va_ref[...], preferred_element_type=F32)
            denominator = summed[:, 128:]
            context = (summed[:, :128] / denominator).astype(BF16)
            level = top + jnp.log2(denominator)
            for g in range(block // group):
                at = r + g * group
                p, inside = at // part, at % part
                out_ref[a, p, inside : inside + group, :] = context[g * group : (g + 1) * group]
                line = jnp.sum(jnp.where(eye, level[g * group : (g + 1) * group], 0.0), axis=0, keepdims=True)
                stat_ref_store(out_ref, a, p, part, inside // group, groups, line)
        return 0

    lax.fori_loop(0, members * each // unroll, body, 0)


def stat_ref_store(out_ref, a, p, part, g, groups, line):
    high = line.astype(BF16)
    rest = line - high.astype(F32)
    middle = rest.astype(BF16)
    low = (rest - middle.astype(F32)).astype(BF16)
    out_ref[a, p, part + g : part + g + 1, :] = high
    out_ref[a, p, part + groups + g : part + groups + g + 1, :] = middle
    out_ref[a, p, part + 2 * groups + g : part + 2 * groups + g + 1, :] = low


def mixing(levels):
    top = functools.reduce(jnp.maximum, levels)
    raw = [jnp.exp2(v - top) for v in levels]
    total = functools.reduce(jnp.add, raw)
    return [v / total for v in raw]


def combined(read_rows, read_stats, members, part):
    group = min(part, 128)
    groups = part // group
    eye = lax.broadcasted_iota(jnp.int32, (group, 128), 0) == lax.broadcasted_iota(jnp.int32, (group, 128), 1)
    levels = []
    for a in range(members):
        stats = read_stats(a).astype(F32)
        levels.append(stats[:groups] + stats[groups : 2 * groups] + stats[2 * groups : 3 * groups])
    shares = mixing(levels)
    out = []
    for g in range(groups):
        total = None
        for a in range(members):
            column = jnp.sum(jnp.where(eye, shares[a][g : g + 1], 0.0), axis=1, keepdims=True)
            term = read_rows(a)[g * group : (g + 1) * group].astype(F32) * column
            total = term if total is None else total + term
        out.append(total)
    return out


def project_out_kernel(info_ref, r_ref, own_ref, mine_ref, theirs_ref, out_ref, ctx_ref, w_ref, sems):
    core = info_ref[0]
    half = D // 2
    copies = started(
        [(own_ref, w_ref.at[:128])]
        + [
            (ref.at[k], w_ref.at[(k + 1) * 128 : (k + 2) * 128, pl.ds(pl.multiple_of(first * half, half), half)])
            for ref, first in ((mine_ref, core), (theirs_ref, 1 - core))
            for k in range(3)
        ],
        sems,
    )
    members, _, full, _ = r_ref.shape
    part = full - 16
    for k in range(4):
        h = info_ref[1 + k]
        pieces = combined(
            lambda a: r_ref[a, h, :part, :], lambda a: r_ref[a, h, part:, :], members, part
        )
        ctx_ref[:, k * 128 : (k + 1) * 128] = pieces[0].astype(BF16)
    wait_for(copies)
    out = jnp.dot(ctx_ref[...], w_ref[...], preferred_element_type=F32).astype(BF16)
    for z in range(4):
        out_ref[z] = out[z * 16 : (z + 1) * 16]


def residual_kernel(r_ref, s_ref, out_ref):
    for j in range(16):
        cols = slice(j * 128, (j + 1) * 128)
        total = s_ref[x_first(j)].astype(F32)
        for z in range(4):
            total = total + r_ref[z, :, cols].astype(F32)
        total = total.astype(BF16)
        for z in range(4):
            out_ref[z, :, cols] = total


def memory_kernel(info_ref, e_ref, gain_ref, mine_ref, theirs_ref, kv_ref, own_ref, norm_ref, e_vmem, w_ref, sems, e_sem):
    core = info_ref[0]
    half = D // 2
    rows = started([(e_ref, e_vmem)], e_sem)
    copies = started(
        [
            (ref.at[h, t], w_ref.at[h, t, pl.ds(pl.multiple_of(first * half, half), half), :])
            for h in range(4)
            for ref, first in ((mine_ref, core), (theirs_ref, 1 - core))
            for t in range(2)
        ],
        sems,
    )
    wait_for(rows)
    for h in range(4):
        at = pl.multiple_of((info_ref[5] * 4 + h) * 128, 128)
        own_ref[h] = e_vmem[:, pl.ds(at, 128)]
    pieces = [e_vmem[:, j * 128 : (j + 1) * 128].astype(F32) for j in range(16)]
    gains = [gain_ref[:, j * 128 : (j + 1) * 128] for j in range(16)]
    for j, n in enumerate(normed_rows(pieces, gains)):
        norm_ref[:, j * 128 : (j + 1) * 128] = n
    for h in range(4):
        wait_for(copies[h * 4 : (h + 1) * 4])
        weights = jnp.concatenate([w_ref[h, 0], w_ref[h, 1]], axis=1)
        out = jnp.dot(norm_ref[...], weights, preferred_element_type=F32).astype(BF16)
        for b in range(4):
            kv_ref[b, h, 0] = out[:, :128]
            kv_ref[b, h, 1] = out[:, 128:]


def finish_kernel(info_ref, r_ref, out_ref):
    members, full, _ = r_ref.shape
    part = full - 16
    pieces = combined(lambda a: r_ref[a, :part, :], lambda a: r_ref[a, part:, :], members, part)
    first, limit = info_ref[0], info_ref[1]
    for g, piece in enumerate(pieces):
        n = piece.shape[0]
        place = first + g * n + lax.broadcasted_iota(jnp.int32, (n, 128), 0)
        out_ref[g * n : (g + 1) * n, :] = jnp.where(place < limit, piece, 0.0).astype(BF16)


def exchange(x, axes):
    return lax.all_to_all(x, axes, 0, 0, tiled=True)


def attend(q, kvs, blocks, info, part, fetched):
    members, rows, _ = q.shape
    keys = len(blocks) * kvs[0].shape[-2]
    return call(
        functools.partial(attend_kernel, part, blocks, fetched),
        shape(members, rows // part, part + 16, 128),
        info,
        q,
        *kvs,
        specs=[SMEM, ANY if fetched else VMEM] + [VMEM] * len(kvs),
        scratch=[pltpu.VMEM((keys, 256), BF16), pltpu.VMEM((keys, 256), BF16)]
        + ([pltpu.VMEM(q.shape, BF16), DMA((1,))] if fetched else []),
        limit=62 if fetched else 48,
        flops=4 * members * rows * keys * 256,
        transcendentals=members * rows * keys,
    )


def swapped(x, axis, size, by):
    return lax.ppermute(x, axis, [(i, i ^ by) for i in range(size)])


def together(*arrays):
    return lax.optimization_barrier(arrays)


def shards(
    source_hidden,
    target_hidden,
    source_length,
    target_length,
    encoder_gain,
    query_weight,
    key_weight,
    value_weight,
    output_weight,
    final_gain,
    cross_query,
    cross_key,
    cross_value,
    cross_gain,
):
    rows = source_hidden.shape[0]
    target_rows = target_hidden.shape[0]
    at = {name: lax.axis_index(name) for name, _ in AXES}
    seq_at = ((at["zl"] * 4 + at["yh"]) * 2 + at["yl"]) * 2 + at["c"]
    quarter = rows // 4
    core_info = jnp.stack([at["c"], at["x"], at["x"] ^ 1, at["x"] ^ 3, at["x"] ^ 2, at["zh"]])

    def first_of(yh):
        return (((at["zl"] * 4 + yh) * 2 + at["yl"]) * 2 + at["c"]) * rows

    key_info = jnp.stack([source_length[0]] + [first_of(at["yh"] ^ k) for k in range(4)])
    memory_info = jnp.stack(
        [source_length[0]] + [first_of(k // 4) + (k % 4) * quarter for k in range(16)]
    )
    target_info = jnp.stack([seq_at * target_rows, target_length[0]])
    gains = [g.reshape(1, D) for g in (encoder_gain, final_gain, cross_gain)]

    half = at["c"] * (D // 2)
    half_weights = jnp.stack([lax.dynamic_slice_in_dim(w, half, D // 2, 0) for w in (cross_key, cross_value)])
    mine = lax.all_gather(half_weights, "x", axis=0)
    source_some = exchange(repeated(source_hidden, 4, 63.9), "zh")
    source_full = exchange(repeated(source_some, 4, 60), "x").reshape(16, rows, 128)
    queries, keys_values = call(
        qkv_kernel,
        (shape(8, rows, 128), shape(2, rows, 128)),
        source_full,
        gains[0],
        query_weight,
        key_weight,
        value_weight,
        specs=[VMEM, VMEM, ANY, ANY, ANY],
        out=(HBM, VMEM),
        scratch=[
            pltpu.VMEM((rows, D), BF16),
            pltpu.VMEM((D, 384), BF16),
            pltpu.VMEM((rows, 128), BF16),
            DMA((3,)),
            DMA((8,)),
        ],
        flops=2 * rows * D * 384,
    )
    queries, target_hidden = together(queries, target_hidden)
    target_hidden, mine = together(target_hidden, mine)
    target_full = lax.all_gather(target_hidden, HEAD, axis=0)
    key_sets = [keys_values] + [swapped(keys_values, "yh", 4, k) for k in (1, 2, 3)]
    queries = exchange(queries, QUERY_GROUP)
    out_half = lax.dynamic_slice_in_dim(output_weight, half, D // 2, 1)
    queries, out_half = together(queries, out_half)
    out_halves = [swapped(out_half, "x", 4, k) for k in (1, 3, 2)]
    partial = attend(queries, key_sets, [(k, ()) for k in range(4)], key_info, quarter, False)
    partial, mine, *out_halves = together(partial, mine, *out_halves)
    out_mine = jnp.stack(out_halves)
    out_theirs = swapped(out_mine, "c", 2, 1)
    partial = exchange(partial.reshape(32, rows // 4 + 16, 128), QUERY_GROUP + ("x",))
    shares = call(
        project_out_kernel,
        shape(4, quarter // 4, D),
        core_info,
        partial.reshape(8, 4, quarter + 16, 128),
        output_weight,
        out_mine,
        out_theirs,
        specs=[SMEM, VMEM] + [ANY] * 3,
        scratch=[pltpu.VMEM((quarter, 512), BF16), pltpu.VMEM((512, D), BF16), DMA((7,))],
        limit=62.5,
        flops=2 * quarter * 512 * D,
    )
    shares = exchange(shares, "zh")
    theirs = swapped(mine, "c", 2, 1)
    shares, theirs = together(shares, theirs)
    first = at["x"] * quarter + at["zh"] * (quarter // 4)
    own_source = lax.dynamic_slice_in_dim(source_full, first, quarter // 4, 1)
    encoder_rows = call(
        residual_kernel, shape(4, quarter // 4, D), shares, own_source, specs=[VMEM] * 2
    )
    encoder_rows = exchange(encoder_rows, "zh").reshape(quarter, D)
    target_queries = call(
        target_kernel,
        shape(target_rows, 128),
        target_full,
        gains[2],
        cross_query,
        specs=[ANY, VMEM, ANY],
        scratch=[
            pltpu.VMEM((target_rows, D), BF16),
            pltpu.VMEM((4, 16, target_rows // 4, 128), BF16),
            pltpu.VMEM((D, 128), BF16),
            DMA((4,)),
            DMA((1,)),
        ],
        flops=2 * target_rows * D * 128,
    )
    encoder_rows, target_queries = together(encoder_rows, target_queries)
    memory, own_columns = call(
        memory_kernel,
        (shape(4, 4, 2, quarter, 128), shape(4, quarter, 128)),
        core_info,
        encoder_rows,
        gains[1],
        mine,
        theirs,
        specs=[SMEM, ANY, VMEM, ANY, ANY],
        scratch=[
            pltpu.VMEM((quarter, D), BF16),
            pltpu.VMEM((quarter, D), BF16),
            pltpu.VMEM((4, 2, D, 128), BF16),
            DMA((16,)),
            DMA((1,)),
        ],
        limit=63,
        flops=2 * quarter * D * 1024,
    )

    target_queries = lax.all_gather(target_queries, QUERY_GROUP, axis=0)
    memory = exchange(memory.reshape(16, 2, quarter, 128), ("yh", "x")).reshape(4, 4, 2, quarter, 128)
    memory, own_columns = together(memory, own_columns)
    encoder_out = exchange(own_columns, "x").reshape(rows, 128)
    crossed = attend(
        target_queries, [memory], [(0, (k // 4, k % 4)) for k in range(16)], memory_info, target_rows, True
    )
    crossed, encoder_out = together(crossed, encoder_out)
    crossed = exchange(crossed.reshape(8, target_rows + 16, 128), QUERY_GROUP)
    cross_context = call(
        finish_kernel, shape(target_rows, 128), target_info, crossed, specs=[SMEM, VMEM]
    )
    return (encoder_out, cross_context)


def solution(mesh):
    fine = Mesh(mesh.devices.reshape([size for _, size in AXES]), [name for name, _ in AXES])
    columns = P(None, HEAD)
    in_specs = (
        P(SEQ, HEAD),
        P(SEQ, HEAD),
        P(),
        P(),
        P(),
        columns,
        columns,
        columns,
        P(HEAD, None),
        P(),
        columns,
        columns,
        columns,
        P(),
    )
    out_specs = (P(SEQ, HEAD), P(SEQ, HEAD))
    return jax.shard_map(shards, mesh=fine, in_specs=in_specs, out_specs=out_specs, check_vma=False)
```

```python
import functools
import math

import jax
import jax.numpy as jnp
from jax import lax
from jax.experimental import pallas as pl
from jax.experimental.pallas import tpu as pltpu
from jax.sharding import Mesh, PartitionSpec as P

HD = 128
D = 2048
EPSILON = 1e-05
MASKED = -1e30
SCORE_SCALE = HD ** (-0.5) * math.log2(math.e)
F32 = jnp.float32
BF16 = jnp.bfloat16

AXES = (("zl", 2), ("yh", 4), ("yl", 2), ("c", 2), ("zh", 4), ("x", 4))
SEQ = ("zl", "yh", "yl", "c")
HEAD = ("zh", "x")
QUERY_GROUP = ("zl", "yl", "c")
VMEM = pl.BlockSpec(memory_space=pltpu.VMEM)
SMEM = pl.BlockSpec(memory_space=pltpu.SMEM)
ANY = pl.BlockSpec(memory_space=pl.ANY)
HBM = pl.BlockSpec(memory_space=pltpu.HBM)
DMA = pltpu.SemaphoreType.DMA


def call(kernel, out_shape, *args, specs, out=None, scratch=(), limit=48, flops=0, transcendentals=0):
    outs = jax.tree.leaves(out_shape)
    size = sum(math.prod(a.shape) * a.dtype.itemsize for a in (*args, *outs))
    return pl.pallas_call(
        kernel,
        out_shape=out_shape,
        in_specs=specs,
        out_specs=jax.tree.map(lambda _: VMEM, out_shape) if out is None else out,
        scratch_shapes=scratch,
        compiler_params=pltpu.CompilerParams(vmem_limit_bytes=int(limit * 1024 * 1024)),
        cost_estimate=pl.CostEstimate(flops=flops, bytes_accessed=size, transcendentals=transcendentals),
    )(*args)


def shape(*dims, dtype=BF16):
    return jax.ShapeDtypeStruct(dims, dtype)


def started(pairs, sems):
    copies = [pltpu.make_async_copy(a, b, sems.at[i]) for i, (a, b) in enumerate(pairs)]
    for copy in copies:
        copy.start()
    return copies


def wait_for(copies):
    for copy in copies:
        copy.wait()


def repeat_kernel(x_ref, out_ref, sems):
    wait_for(started([(x_ref, out_ref.at[i]) for i in range(out_ref.shape[0])], sems))


def repeated(x, times):
    return call(
        repeat_kernel, shape(times, *x.shape), x, specs=[VMEM], out=HBM, scratch=[DMA((times,))], limit=63.9
    )


def normed_rows(pieces, gains):
    total = functools.reduce(jnp.add, pieces)
    mean = jnp.sum(total, axis=-1, keepdims=True) * (1.0 / D)
    centers = [p - mean for p in pieces]
    squares = functools.reduce(jnp.add, [c * c for c in centers])
    spread = jnp.sum(squares, axis=-1, keepdims=True) * (1.0 / D)
    inverse = lax.rsqrt(spread + EPSILON)
    return [(c * inverse * g).astype(BF16) for c, g in zip(centers, gains)]


def norm_gathered(x_ref, gain_ref, norm_ref, step=64):
    rows = x_ref.shape[1]

    def body(i, _):
        r = pl.multiple_of(i * step, step)
        pieces = [x_ref[j, pl.ds(r, step), :].astype(F32) for j in range(16)]
        gains = [gain_ref[:, j * 128 : (j + 1) * 128] for j in range(16)]
        for j, n in enumerate(normed_rows(pieces, gains)):
            norm_ref[pl.ds(r, step), j * 128 : (j + 1) * 128] = n
        return 0

    lax.fori_loop(0, rows // step, body, 0)


def qkv_kernel(x_ref, gain_ref, wq_ref, wk_ref, wv_ref, q_ref, kv_ref, norm_ref, w_ref, kv_one_ref, in_sems, out_sems):
    weights = started(
        [(w, w_ref.at[:, i * 128 : (i + 1) * 128]) for i, w in enumerate((wq_ref, wk_ref, wv_ref))], in_sems
    )
    norm_gathered(x_ref, gain_ref, norm_ref)
    wait_for(weights)
    out = jnp.dot(norm_ref[...], w_ref[...], preferred_element_type=F32)
    kv_one_ref[0] = out[:, 128:256].astype(BF16)
    kv_one_ref[1] = out[:, 256:].astype(BF16)
    copies = started([(kv_one_ref, kv_ref.at[b]) for b in range(kv_ref.shape[0])], out_sems)
    q_ref[...] = (out[:, :128] * SCORE_SCALE).astype(BF16)
    wait_for(copies)


def target_kernel(x_ref, gain_ref, wq_ref, q_ref, norm_ref, x_vmem, w_ref, x_sems, w_sem):
    rows = x_ref.shape[1]
    parts = x_vmem.shape[0]
    step = rows // parts
    weights = started([(wq_ref, w_ref)], w_sem)
    pieces = started(
        [(x_ref.at[:, i * step : (i + 1) * step, :], x_vmem.at[i]) for i in range(parts)], x_sems
    )
    for i, piece in enumerate(pieces):
        piece.wait()
        norm_gathered(x_vmem.at[i], gain_ref, norm_ref.at[i * step : (i + 1) * step, :])
    wait_for(weights)
    out = jnp.dot(norm_ref[...], w_ref[...], preferred_element_type=F32)
    q_ref[...] = (out * SCORE_SCALE).astype(BF16)


def attend_kernel(part, blocks, fetched, split, info_ref, *refs):
    q_refs, refs = refs[:split], refs[split:]
    q_ref = q_refs[0]
    kv_refs, (out_ref, ka_ref, va_ref, *q_scratch) = refs[: len(refs) - 3 - fetched * 2], refs[len(refs) - 3 - fetched * 2 :]
    rows = q_ref.shape[-2]
    members = split if split > 1 else q_ref.shape[0]
    q_vmem, q_copy = q_ref, []
    if fetched:
        q_vmem, q_sem = q_scratch
        q_copy = started([(q_ref, q_vmem)], q_sem)
    limit = info_ref[0]
    n = kv_refs[0].shape[-2]
    lane = lax.broadcasted_iota(jnp.int32, (n, 128), 1)
    row = lax.broadcasted_iota(jnp.int32, (n, 128), 0)
    for b, (ref, at) in enumerate(blocks):
        place = info_ref[1 + b] + row
        bias = jnp.where((lane == 0) & (place >= limit), MASKED, 0.0).astype(BF16)
        here = slice(b * n, (b + 1) * n)
        ka_ref[here, :128] = kv_refs[ref][(*at, 0)]
        ka_ref[here, 128:] = bias
        va_ref[here, :128] = kv_refs[ref][(*at, 1)]
        va_ref[here, 128:] = jnp.ones((n, 128), BF16)
    ones = jnp.where(lax.broadcasted_iota(jnp.int32, (256, 128), 1) == 0, 1.0, 0.0).astype(BF16)
    group = min(part, 128)
    groups = part // group
    eye = lax.broadcasted_iota(jnp.int32, (group, 128), 0) == lax.broadcasted_iota(jnp.int32, (group, 128), 1)
    block = 256
    each = rows // block
    unroll = min(8, members * each)

    wait_for(q_copy)

    def body(i, _):
        for u in range(unroll):
            step = i * unroll + u
            a, r = (step, 0) if each == 1 else (step // each, (u % each) * block)
            if split > 1:
                q = q_refs[u // each][r : r + block, :]
                a = info_ref[1 + len(blocks) + u // each]
            else:
                q = q_vmem[a, pl.ds(r, block), :]
            q = jnp.concatenate([q, ones], axis=1)
            scores = lax.dot_general(q, ka_ref[...], (((1,), (1,)), ((), ())), preferred_element_type=F32)
            top = jnp.max(scores, axis=1, keepdims=True)
            weights = jnp.exp2(scores - top).astype(BF16)
            summed = jnp.dot(weights, va_ref[...], preferred_element_type=F32)
            denominator = summed[:, 128:]
            context = (summed[:, :128] / denominator).astype(BF16)
            level = top + jnp.log2(denominator)
            for g in range(block // group):
                at = r + g * group
                p, inside = at // part, at % part
                out_ref[a, p, inside : inside + group, :] = context[g * group : (g + 1) * group]
                line = jnp.sum(jnp.where(eye, level[g * group : (g + 1) * group], 0.0), axis=0, keepdims=True)
                stat_ref_store(out_ref, a, p, part, inside // group, groups, line)
        return 0

    lax.fori_loop(0, members * each // unroll, body, 0)


def stat_ref_store(out_ref, a, p, part, g, groups, line):
    high = line.astype(BF16)
    rest = line - high.astype(F32)
    middle = rest.astype(BF16)
    low = (rest - middle.astype(F32)).astype(BF16)
    out_ref[a, p, part + g : part + g + 1, :] = high
    out_ref[a, p, part + groups + g : part + groups + g + 1, :] = middle
    out_ref[a, p, part + 2 * groups + g : part + 2 * groups + g + 1, :] = low


def mixing(levels):
    top = functools.reduce(jnp.maximum, levels)
    raw = [jnp.exp2(v - top) for v in levels]
    total = functools.reduce(jnp.add, raw)
    return [v / total for v in raw]


def combined(read_rows, read_stats, members, part):
    group = min(part, 128)
    groups = part // group
    eye = lax.broadcasted_iota(jnp.int32, (group, 128), 0) == lax.broadcasted_iota(jnp.int32, (group, 128), 1)
    levels = []
    for a in range(members):
        stats = read_stats(a).astype(F32)
        levels.append(stats[:groups] + stats[groups : 2 * groups] + stats[2 * groups : 3 * groups])
    shares = mixing(levels)
    out = []
    for g in range(groups):
        total = None
        for a in range(members):
            column = jnp.sum(jnp.where(eye, shares[a][g : g + 1], 0.0), axis=1, keepdims=True)
            term = read_rows(a)[g * group : (g + 1) * group].astype(F32) * column
            total = term if total is None else total + term
        out.append(total)
    return out


def project_out_kernel(info_ref, r_ref, own_ref, mine_ref, theirs_ref, out_ref, ctx_ref, w_ref, sems):
    core = info_ref[0]
    half = D // 2
    copies = started(
        [(own_ref, w_ref.at[:128])]
        + [
            (ref.at[k], w_ref.at[(k + 1) * 128 : (k + 2) * 128, pl.ds(pl.multiple_of(first * half, half), half)])
            for ref, first in ((mine_ref, core), (theirs_ref, 1 - core))
            for k in range(3)
        ],
        sems,
    )
    members, _, full, _ = r_ref.shape
    part = full - 16
    for k in range(4):
        h = info_ref[1 + k]
        pieces = combined(
            lambda a: r_ref[a, h, :part, :], lambda a: r_ref[a, h, part:, :], members, part
        )
        ctx_ref[:, k * 128 : (k + 1) * 128] = pieces[0].astype(BF16)
    wait_for(copies)
    out = jnp.dot(ctx_ref[...], w_ref[...], preferred_element_type=F32).astype(BF16)
    for z in range(4):
        out_ref[z] = out[z * 16 : (z + 1) * 16]


def residual_kernel(r_ref, s_ref, out_ref):
    for j in range(16):
        cols = slice(j * 128, (j + 1) * 128)
        total = s_ref[j].astype(F32)
        for z in range(4):
            total = total + r_ref[z, :, cols].astype(F32)
        total = total.astype(BF16)
        for z in range(4):
            out_ref[z, :, cols] = total


def memory_kernel(info_ref, e_ref, gain_ref, mine_ref, theirs_ref, kv_ref, norm_ref, e_vmem, w_ref, sems, e_sem):
    core = info_ref[0]
    half = D // 2
    rows = started([(e_ref, e_vmem)], e_sem)
    copies = started(
        [
            (ref.at[h, t], w_ref.at[h, pl.ds(pl.multiple_of(first * half, half), half), t * 128 : (t + 1) * 128])
            for h in range(4)
            for ref, first in ((mine_ref, core), (theirs_ref, 1 - core))
            for t in range(2)
        ],
        sems,
    )
    wait_for(rows)
    pieces = [e_vmem[:, j * 128 : (j + 1) * 128].astype(F32) for j in range(16)]
    gains = [gain_ref[:, j * 128 : (j + 1) * 128] for j in range(16)]
    for j, n in enumerate(normed_rows(pieces, gains)):
        norm_ref[:, j * 128 : (j + 1) * 128] = n
    for h in range(4):
        wait_for(copies[h * 4 : (h + 1) * 4])
        out = jnp.dot(norm_ref[...], w_ref[h], preferred_element_type=F32).astype(BF16)
        for b in range(4):
            kv_ref[b, h, 0] = out[:, :128]
            kv_ref[b, h, 1] = out[:, 128:]


def finish_kernel(info_ref, r_ref, out_ref):
    members, full, _ = r_ref.shape
    part = full - 16
    pieces = combined(lambda a: r_ref[a, :part, :], lambda a: r_ref[a, part:, :], members, part)
    first, limit = info_ref[0], info_ref[1]
    for g, piece in enumerate(pieces):
        n = piece.shape[0]
        place = first + g * n + lax.broadcasted_iota(jnp.int32, (n, 128), 0)
        out_ref[g * n : (g + 1) * n, :] = jnp.where(place < limit, piece, 0.0).astype(BF16)


def exchange(x, axes):
    return lax.all_to_all(x, axes, 0, 0, tiled=True)


def attend(qs, kvs, blocks, info, part, fetched):
    split = len(qs)
    rows = qs[0].shape[-2]
    members = split if split > 1 else qs[0].shape[0]
    keys = len(blocks) * kvs[0].shape[-2]
    return call(
        functools.partial(attend_kernel, part, blocks, fetched, split),
        shape(members, rows // part, part + 16, 128),
        info,
        *qs,
        *kvs,
        specs=[SMEM] + [ANY if fetched else VMEM] * split + [VMEM] * len(kvs),
        scratch=[pltpu.VMEM((keys, 256), BF16), pltpu.VMEM((keys, 256), BF16)]
        + ([pltpu.VMEM(qs[0].shape, BF16), DMA((1,))] if fetched else []),
        limit=62 if fetched else 48,
        flops=4 * members * rows * keys * 256,
        transcendentals=members * rows * keys,
    )


def swapped(x, axis, size, by):
    return lax.ppermute(x, axis, [(i, i ^ by) for i in range(size)])


def together(*arrays):
    return lax.optimization_barrier(arrays)


def shards(
    source_hidden,
    target_hidden,
    source_length,
    target_length,
    encoder_gain,
    query_weight,
    key_weight,
    value_weight,
    output_weight,
    final_gain,
    cross_query,
    cross_key,
    cross_value,
    cross_gain,
):
    rows = source_hidden.shape[0]
    target_rows = target_hidden.shape[0]
    at = {name: lax.axis_index(name) for name, _ in AXES}
    seq_at = ((at["zl"] * 4 + at["yh"]) * 2 + at["yl"]) * 2 + at["c"]
    quarter = rows // 4
    core_info = jnp.stack([at["c"], at["x"], at["x"] ^ 1, at["x"] ^ 3, at["x"] ^ 2])

    def first_of(yh):
        return (((at["zl"] * 4 + yh) * 2 + at["yl"]) * 2 + at["c"]) * rows

    key_info = jnp.stack(
        [source_length[0]]
        + [(((k // 4 * 4 + at["yh"]) * 2 + k // 2 % 2) * 2 + k % 2) * rows for k in range(8)]
        + [at["yh"] ^ k for k in range(4)]
    )
    memory_info = jnp.stack(
        [source_length[0]] + [first_of(k // 4) + (k % 4) * quarter for k in range(16)]
    )
    target_info = jnp.stack([seq_at * target_rows, target_length[0]])
    gains = [g.reshape(1, D) for g in (encoder_gain, final_gain, cross_gain)]

    half = at["c"] * (D // 2)
    out_half = lax.dynamic_slice_in_dim(output_weight, half, D // 2, 1)
    out_halves = [swapped(out_half, "x", 4, k) for k in (1, 3)]
    target_full = lax.all_gather(target_hidden, HEAD, axis=0)
    source_full = exchange(repeated(source_hidden, 16), HEAD)
    source_full, *out_halves = together(source_full, *out_halves)
    out_halves.append(swapped(out_halves[0], "x", 4, 3))
    half_weights = jnp.stack([lax.dynamic_slice_in_dim(w, half, D // 2, 0) for w in (cross_key, cross_value)])
    source_full, half_weights = together(source_full, half_weights)
    mine = lax.all_gather(half_weights, "x", axis=0)

    queries, keys_values = call(
        qkv_kernel,
        (shape(rows, 128), shape(8, 2, rows, 128)),
        source_full,
        gains[0],
        query_weight,
        key_weight,
        value_weight,
        specs=[VMEM, VMEM, ANY, ANY, ANY],
        out=(VMEM, HBM),
        scratch=[
            pltpu.VMEM((rows, D), BF16),
            pltpu.VMEM((D, 384), BF16),
            pltpu.VMEM((2, rows, 128), BF16),
            DMA((3,)),
            DMA((8,)),
        ],
        flops=2 * rows * D * 384,
    )
    queries = [queries] + [swapped(queries, "yh", 4, k) for k in (1, 2, 3)]
    keys_values = exchange(keys_values, QUERY_GROUP).reshape(8, 1, 2, rows, 128)
    keys_values, out_halves[2] = together(keys_values, out_halves[2])
    out_mine = jnp.stack(out_halves)
    out_theirs = swapped(out_mine, "c", 2, 1)
    partial = attend(queries, [keys_values], [(0, (k, 0)) for k in range(8)], key_info, quarter, False)
    partial = exchange(partial.reshape(16, rows // 4 + 16, 128), ("yh", "x"))
    target_queries = call(
        target_kernel,
        shape(target_rows, 128),
        target_full,
        gains[2],
        cross_query,
        specs=[ANY, VMEM, ANY],
        scratch=[
            pltpu.VMEM((target_rows, D), BF16),
            pltpu.VMEM((4, 16, target_rows // 4, 128), BF16),
            pltpu.VMEM((D, 128), BF16),
            DMA((4,)),
            DMA((1,)),
        ],
        flops=2 * target_rows * D * 128,
    )
    partial, target_queries = together(partial, target_queries)
    shares = call(
        project_out_kernel,
        shape(4, quarter // 4, D),
        core_info,
        partial.reshape(4, 4, quarter + 16, 128),
        output_weight,
        out_mine,
        out_theirs,
        specs=[SMEM, VMEM] + [ANY] * 3,
        scratch=[pltpu.VMEM((quarter, 512), BF16), pltpu.VMEM((512, D), BF16), DMA((7,))],
        limit=62.5,
        flops=2 * quarter * 512 * D,
    )
    shares = exchange(shares, "zh")
    shares, mine = together(shares, mine)
    theirs = swapped(mine, "c", 2, 1)
    first = at["x"] * quarter + at["zh"] * (quarter // 4)
    own_source = lax.dynamic_slice_in_dim(source_full, first, quarter // 4, 1)
    encoder_rows = call(
        residual_kernel, shape(4, quarter // 4, D), shares, own_source, specs=[VMEM] * 2
    )
    encoder_rows = exchange(encoder_rows, "zh").reshape(quarter, D)
    memory = call(
        memory_kernel,
        shape(4, 4, 2, quarter, 128),
        core_info,
        encoder_rows,
        gains[1],
        mine,
        theirs,
        specs=[SMEM, ANY, VMEM, ANY, ANY],
        scratch=[
            pltpu.VMEM((quarter, D), BF16),
            pltpu.VMEM((quarter, D), BF16),
            pltpu.VMEM((4, D, 256), BF16),
            DMA((16,)),
            DMA((1,)),
        ],
        limit=63,
        flops=2 * quarter * D * 1024,
    )
    encoder_full = lax.all_gather(encoder_rows, "x", axis=0, tiled=True)

    target_queries = lax.all_gather(target_queries, QUERY_GROUP, axis=0)
    memory = exchange(memory.reshape(16, 2, quarter, 128), ("yh", "x")).reshape(4, 4, 2, quarter, 128)
    crossed = attend(
        [target_queries], [memory], [(0, (k // 4, k % 4)) for k in range(16)], memory_info, target_rows, True
    )
    crossed, encoder_full = together(crossed, encoder_full)
    crossed = exchange(crossed.reshape(8, target_rows + 16, 128), QUERY_GROUP)
    head_at = at["zh"] * 4 + at["x"]
    encoder_out = lax.dynamic_slice_in_dim(encoder_full, head_at * 128, 128, 1)
    cross_context = call(
        finish_kernel, shape(target_rows, 128), target_info, crossed, specs=[SMEM, VMEM]
    )
    return (encoder_out, cross_context)


def solution(mesh):
    fine = Mesh(mesh.devices.reshape([size for _, size in AXES]), [name for name, _ in AXES])
    columns = P(None, HEAD)
    in_specs = (
        P(SEQ, HEAD),
        P(SEQ, HEAD),
        P(),
        P(),
        P(),
        columns,
        columns,
        columns,
        P(HEAD, None),
        P(),
        columns,
        columns,
        columns,
        P(),
    )
    out_specs = (P(SEQ, HEAD), P(SEQ, HEAD))
    return jax.shard_map(shards, mesh=fine, in_specs=in_specs, out_specs=out_specs, check_vma=False)
```

```python
import functools
import math

import jax
import jax.numpy as jnp
from jax import lax
from jax.experimental import pallas as pl
from jax.experimental.pallas import tpu as pltpu
from jax.sharding import Mesh, PartitionSpec as P

HD = 128
D = 2048
EPSILON = 1e-05
MASKED = -1e30
SCORE_SCALE = HD ** (-0.5) * math.log2(math.e)
F32 = jnp.float32
BF16 = jnp.bfloat16

AXES = (("zl", 2), ("yh", 4), ("yl", 2), ("c", 2), ("zh", 4), ("x", 4))
SEQ = ("zl", "yh", "yl", "c")
HEAD = ("zh", "x")
QUERY_GROUP = ("zl", "yl", "c")
VMEM = pl.BlockSpec(memory_space=pltpu.VMEM)
SMEM = pl.BlockSpec(memory_space=pltpu.SMEM)
ANY = pl.BlockSpec(memory_space=pl.ANY)
HBM = pl.BlockSpec(memory_space=pltpu.HBM)
DMA = pltpu.SemaphoreType.DMA


def call(kernel, out_shape, *args, specs, out=None, scratch=(), limit=48, flops=0, transcendentals=0):
    outs = jax.tree.leaves(out_shape)
    size = sum(math.prod(a.shape) * a.dtype.itemsize for a in (*args, *outs))
    return pl.pallas_call(
        kernel,
        out_shape=out_shape,
        in_specs=specs,
        out_specs=jax.tree.map(lambda _: VMEM, out_shape) if out is None else out,
        scratch_shapes=scratch,
        compiler_params=pltpu.CompilerParams(vmem_limit_bytes=int(limit * 1024 * 1024)),
        cost_estimate=pl.CostEstimate(flops=flops, bytes_accessed=size, transcendentals=transcendentals),
    )(*args)


def shape(*dims, dtype=BF16):
    return jax.ShapeDtypeStruct(dims, dtype)


def started(pairs, sems):
    copies = [pltpu.make_async_copy(a, b, sems.at[i]) for i, (a, b) in enumerate(pairs)]
    for copy in copies:
        copy.start()
    return copies


def wait_for(copies):
    for copy in copies:
        copy.wait()


def repeat_kernel(x_ref, out_ref, sems):
    wait_for(started([(x_ref, out_ref.at[i]) for i in range(out_ref.shape[0])], sems))


def repeated(x, times):
    return call(
        repeat_kernel, shape(times, *x.shape), x, specs=[VMEM], out=HBM, scratch=[DMA((times,))], limit=63.9
    )


def normed_rows(pieces, gains):
    total = functools.reduce(jnp.add, pieces)
    mean = jnp.sum(total, axis=-1, keepdims=True) * (1.0 / D)
    centers = [p - mean for p in pieces]
    squares = functools.reduce(jnp.add, [c * c for c in centers])
    spread = jnp.sum(squares, axis=-1, keepdims=True) * (1.0 / D)
    inverse = lax.rsqrt(spread + EPSILON)
    return [(c * inverse * g).astype(BF16) for c, g in zip(centers, gains)]


def norm_gathered(x_ref, gain_ref, norm_ref, step=64):
    rows = x_ref.shape[1]

    def body(i, _):
        r = pl.multiple_of(i * step, step)
        pieces = [x_ref[j, pl.ds(r, step), :].astype(F32) for j in range(16)]
        gains = [gain_ref[:, j * 128 : (j + 1) * 128] for j in range(16)]
        for j, n in enumerate(normed_rows(pieces, gains)):
            norm_ref[pl.ds(r, step), j * 128 : (j + 1) * 128] = n
        return 0

    lax.fori_loop(0, rows // step, body, 0)


def qkv_kernel(x_ref, gain_ref, wq_ref, wk_ref, wv_ref, q_ref, kv_ref, norm_ref, w_ref, q_one_ref, in_sems, out_sems):
    weights = started(
        [(w, w_ref.at[:, i * 128 : (i + 1) * 128]) for i, w in enumerate((wq_ref, wk_ref, wv_ref))], in_sems
    )
    norm_gathered(x_ref, gain_ref, norm_ref)
    wait_for(weights)
    out = jnp.dot(norm_ref[...], w_ref[...], preferred_element_type=F32)
    q_one_ref[...] = (out[:, :128] * SCORE_SCALE).astype(BF16)
    copies = started([(q_one_ref, q_ref.at[a]) for a in range(q_ref.shape[0])], out_sems)
    kv_ref[0] = out[:, 128:256].astype(BF16)
    kv_ref[1] = out[:, 256:].astype(BF16)
    wait_for(copies)


def target_kernel(x_ref, gain_ref, wq_ref, q_ref, norm_ref, x_vmem, w_ref, x_sems, w_sem):
    rows = x_ref.shape[1]
    parts = x_vmem.shape[0]
    step = rows // parts
    weights = started([(wq_ref, w_ref)], w_sem)
    pieces = started(
        [(x_ref.at[:, i * step : (i + 1) * step, :], x_vmem.at[i]) for i in range(parts)], x_sems
    )
    for i, piece in enumerate(pieces):
        piece.wait()
        norm_gathered(x_vmem.at[i], gain_ref, norm_ref.at[i * step : (i + 1) * step, :])
    wait_for(weights)
    out = jnp.dot(norm_ref[...], w_ref[...], preferred_element_type=F32)
    q_ref[...] = (out * SCORE_SCALE).astype(BF16)


def attend_kernel(part, blocks, fetched, info_ref, q_ref, *refs):
    kv_refs, (out_ref, ka_ref, va_ref, *q_scratch) = refs[: len(refs) - 3 - fetched * 4], refs[len(refs) - 3 - fetched * 4 :]
    members, rows, _ = q_ref.shape
    q_vmem, q_copy = q_ref, []
    if fetched:
        q_vmem, out_vmem, q_sem, out_sem = q_scratch
        q_copy = started([(q_ref.at[a], q_vmem.at[a]) for a in range(members)], q_sem)
        out_ref, out_hbm = out_vmem, out_ref
    limit = info_ref[0]
    n = kv_refs[0].shape[-2]
    lane = lax.broadcasted_iota(jnp.int32, (n, 128), 1)
    row = lax.broadcasted_iota(jnp.int32, (n, 128), 0)
    for b, (ref, at) in enumerate(blocks):
        place = info_ref[1 + b] + row
        bias = jnp.where((lane == 0) & (place >= limit), MASKED, 0.0).astype(BF16)
        here = slice(b * n, (b + 1) * n)
        ka_ref[here, :128] = kv_refs[ref][(*at, 0)]
        ka_ref[here, 128:] = bias
        va_ref[here, :128] = kv_refs[ref][(*at, 1)]
        va_ref[here, 128:] = jnp.ones((n, 128), BF16)
    ones = jnp.where(lax.broadcasted_iota(jnp.int32, (256, 128), 1) == 0, 1.0, 0.0).astype(BF16)
    group = min(part, 128)
    groups = part // group
    eye = lax.broadcasted_iota(jnp.int32, (group, 128), 0) == lax.broadcasted_iota(jnp.int32, (group, 128), 1)
    block = 256
    each = rows // block
    unroll = 8

    def body(i, _):
        for u in range(unroll):
            step = i * unroll + u
            a, r = (step, 0) if each == 1 else (step // each, (u % each) * block)
            q = jnp.concatenate([q_vmem[a, pl.ds(r, block), :], ones], axis=1)
            scores = lax.dot_general(q, ka_ref[...], (((1,), (1,)), ((), ())), preferred_element_type=F32)
            top = jnp.max(scores, axis=1, keepdims=True)
            weights = jnp.exp2(scores - top).astype(BF16)
            summed = jnp.dot(weights, va_ref[...], preferred_element_type=F32)
            denominator = summed[:, 128:]
            context = (summed[:, :128] / denominator).astype(BF16)
            level = top + jnp.log2(denominator)
            for g in range(block // group):
                at = r + g * group
                p, inside = at // part, at % part
                out_ref[a, p, inside : inside + group, :] = context[g * group : (g + 1) * group]
                line = jnp.sum(jnp.where(eye, level[g * group : (g + 1) * group], 0.0), axis=0, keepdims=True)
                stat_ref_store(out_ref, a, p, part, inside // group, groups, line)
        return 0

    if not fetched:
        lax.fori_loop(0, members * each // unroll, body, 0)
        return
    out_copies = []
    for i in range(members * each // unroll):
        done = range(i * unroll // each, (i + 1) * unroll // each)
        wait_for([q_copy[a] for a in done])
        body(i, 0)
        out_copies += [pltpu.make_async_copy(out_ref.at[a], out_hbm.at[a], out_sem.at[a]) for a in done]
        for copy in out_copies[-len(done) :]:
            copy.start()
    wait_for(out_copies)


def stat_ref_store(out_ref, a, p, part, g, groups, line):
    high = line.astype(BF16)
    rest = line - high.astype(F32)
    middle = rest.astype(BF16)
    low = (rest - middle.astype(F32)).astype(BF16)
    out_ref[a, p, part + g : part + g + 1, :] = high
    out_ref[a, p, part + groups + g : part + groups + g + 1, :] = middle
    out_ref[a, p, part + 2 * groups + g : part + 2 * groups + g + 1, :] = low


def mixing(levels):
    top = functools.reduce(jnp.maximum, levels)
    raw = [jnp.exp2(v - top) for v in levels]
    total = functools.reduce(jnp.add, raw)
    return [v / total for v in raw]


def combined(read_rows, read_stats, members, part):
    group = min(part, 128)
    groups = part // group
    eye = lax.broadcasted_iota(jnp.int32, (group, 128), 0) == lax.broadcasted_iota(jnp.int32, (group, 128), 1)
    levels = []
    for a in range(members):
        stats = read_stats(a).astype(F32)
        levels.append(stats[:groups] + stats[groups : 2 * groups] + stats[2 * groups : 3 * groups])
    shares = mixing(levels)
    out = []
    for g in range(groups):
        total = None
        for a in range(members):
            column = jnp.sum(jnp.where(eye, shares[a][g : g + 1], 0.0), axis=1, keepdims=True)
            term = read_rows(a)[g * group : (g + 1) * group].astype(F32) * column
            total = term if total is None else total + term
        out.append(total)
    return out


def project_out_kernel(info_ref, r_ref, own_ref, mine_ref, theirs_ref, out_ref, ctx_ref, w_ref, sems):
    core = info_ref[0]
    half = D // 2
    copies = started(
        [(own_ref, w_ref.at[:128])]
        + [
            (ref.at[k], w_ref.at[(k + 1) * 128 : (k + 2) * 128, pl.ds(pl.multiple_of(first * half, half), half)])
            for ref, first in ((mine_ref, core), (theirs_ref, 1 - core))
            for k in range(3)
        ],
        sems,
    )
    members, _, full, _ = r_ref.shape
    part = full - 16
    for k in range(4):
        h = info_ref[1 + k]
        pieces = combined(
            lambda a: r_ref[a, h, :part, :], lambda a: r_ref[a, h, part:, :], members, part
        )
        ctx_ref[:, k * 128 : (k + 1) * 128] = pieces[0].astype(BF16)
    wait_for(copies)
    out = jnp.dot(ctx_ref[...], w_ref[...], preferred_element_type=F32).astype(BF16)
    for z in range(4):
        out_ref[z] = out[z * 16 : (z + 1) * 16]


def residual_kernel(r_ref, s_ref, out_ref):
    for j in range(16):
        cols = slice(j * 128, (j + 1) * 128)
        total = s_ref[j].astype(F32)
        for z in range(4):
            total = total + r_ref[z, :, cols].astype(F32)
        total = total.astype(BF16)
        for z in range(4):
            out_ref[z, :, cols] = total


def memory_kernel(info_ref, e_ref, gain_ref, mine_ref, theirs_ref, kv_ref, norm_ref, e_vmem, w_ref, sems, e_sem):
    core = info_ref[0]
    half = D // 2
    rows = started([(e_ref, e_vmem)], e_sem)
    copies = started(
        [
            (ref.at[h, t], w_ref.at[h, pl.ds(pl.multiple_of(first * half, half), half), t * 128 : (t + 1) * 128])
            for h in range(4)
            for ref, first in ((mine_ref, core), (theirs_ref, 1 - core))
            for t in range(2)
        ],
        sems,
    )
    wait_for(rows)
    pieces = [e_vmem[:, j * 128 : (j + 1) * 128].astype(F32) for j in range(16)]
    gains = [gain_ref[:, j * 128 : (j + 1) * 128] for j in range(16)]
    for j, n in enumerate(normed_rows(pieces, gains)):
        norm_ref[:, j * 128 : (j + 1) * 128] = n
    for h in range(4):
        wait_for(copies[h * 4 : (h + 1) * 4])
        out = jnp.dot(norm_ref[...], w_ref[h], preferred_element_type=F32).astype(BF16)
        for b in range(4):
            kv_ref[b, h, 0] = out[:, :128]
            kv_ref[b, h, 1] = out[:, 128:]


def finish_kernel(info_ref, r_ref, out_ref):
    members, full, _ = r_ref.shape
    part = full - 16
    pieces = combined(lambda a: r_ref[a, :part, :], lambda a: r_ref[a, part:, :], members, part)
    first, limit = info_ref[0], info_ref[1]
    for g, piece in enumerate(pieces):
        n = piece.shape[0]
        place = first + g * n + lax.broadcasted_iota(jnp.int32, (n, 128), 0)
        out_ref[g * n : (g + 1) * n, :] = jnp.where(place < limit, piece, 0.0).astype(BF16)


def exchange(x, axes):
    return lax.all_to_all(x, axes, 0, 0, tiled=True)


def attend(q, kvs, blocks, info, part, fetched):
    members, rows, _ = q.shape
    keys = len(blocks) * kvs[0].shape[-2]
    return call(
        functools.partial(attend_kernel, part, blocks, fetched),
        shape(members, rows // part, part + 16, 128),
        info,
        q,
        *kvs,
        specs=[SMEM, ANY if fetched else VMEM] + [VMEM] * len(kvs),
        scratch=[pltpu.VMEM((keys, 256), BF16), pltpu.VMEM((keys, 256), BF16)]
        + (
            [
                pltpu.VMEM(q.shape, BF16),
                pltpu.VMEM((members, rows // part, part + 16, 128), BF16),
                DMA((members,)),
                DMA((members,)),
            ]
            if fetched
            else []
        ),
        out=HBM if fetched else None,
        limit=62 if fetched else 48,
        flops=4 * members * rows * keys * 256,
        transcendentals=members * rows * keys,
    )


def swapped(x, axis, size, by):
    return lax.ppermute(x, axis, [(i, i ^ by) for i in range(size)])


def together(*arrays):
    return lax.optimization_barrier(arrays)


def shards(
    source_hidden,
    target_hidden,
    source_length,
    target_length,
    encoder_gain,
    query_weight,
    key_weight,
    value_weight,
    output_weight,
    final_gain,
    cross_query,
    cross_key,
    cross_value,
    cross_gain,
):
    rows = source_hidden.shape[0]
    target_rows = target_hidden.shape[0]
    at = {name: lax.axis_index(name) for name, _ in AXES}
    seq_at = ((at["zl"] * 4 + at["yh"]) * 2 + at["yl"]) * 2 + at["c"]
    quarter = rows // 4
    core_info = jnp.stack([at["c"], at["x"], at["x"] ^ 1, at["x"] ^ 3, at["x"] ^ 2])

    def first_of(yh):
        return (((at["zl"] * 4 + yh) * 2 + at["yl"]) * 2 + at["c"]) * rows

    key_info = jnp.stack([source_length[0]] + [first_of(at["yh"] ^ k) for k in range(4)])
    memory_info = jnp.stack(
        [source_length[0]] + [first_of(k // 4) + (k % 4) * quarter for k in range(16)]
    )
    target_info = jnp.stack([seq_at * target_rows, target_length[0]])
    gains = [g.reshape(1, D) for g in (encoder_gain, final_gain, cross_gain)]

    half = at["c"] * (D // 2)
    target_full = lax.all_gather(target_hidden, HEAD, axis=0)
    source_full = exchange(repeated(source_hidden, 16), HEAD)
    half_weights = jnp.stack([lax.dynamic_slice_in_dim(w, half, D // 2, 0) for w in (cross_key, cross_value)])
    source_full, half_weights = together(source_full, half_weights)
    mine = lax.all_gather(half_weights, "x", axis=0)

    queries, keys_values = call(
        qkv_kernel,
        (shape(8, rows, 128), shape(2, rows, 128)),
        source_full,
        gains[0],
        query_weight,
        key_weight,
        value_weight,
        specs=[VMEM, VMEM, ANY, ANY, ANY],
        out=(HBM, VMEM),
        scratch=[
            pltpu.VMEM((rows, D), BF16),
            pltpu.VMEM((D, 384), BF16),
            pltpu.VMEM((rows, 128), BF16),
            DMA((3,)),
            DMA((8,)),
        ],
        flops=2 * rows * D * 384,
    )
    key_sets = [keys_values] + [swapped(keys_values, "yh", 4, k) for k in (1, 2, 3)]
    queries = exchange(queries, QUERY_GROUP)
    out_half = lax.dynamic_slice_in_dim(output_weight, half, D // 2, 1)
    queries, out_half = together(queries, out_half)
    out_halves = [swapped(out_half, "x", 4, k) for k in (1, 3, 2)]
    partial = attend(queries, key_sets, [(k, ()) for k in range(4)], key_info, quarter, False)
    partial, *out_halves = together(partial, *out_halves)
    out_mine = jnp.stack(out_halves)
    out_theirs = swapped(out_mine, "c", 2, 1)
    partial = exchange(partial.reshape(32, rows // 4 + 16, 128), QUERY_GROUP + ("x",))
    target_queries = call(
        target_kernel,
        shape(target_rows, 128),
        target_full,
        gains[2],
        cross_query,
        specs=[ANY, VMEM, ANY],
        scratch=[
            pltpu.VMEM((target_rows, D), BF16),
            pltpu.VMEM((4, 16, target_rows // 4, 128), BF16),
            pltpu.VMEM((D, 128), BF16),
            DMA((4,)),
            DMA((1,)),
        ],
        flops=2 * target_rows * D * 128,
    )
    partial, target_queries = together(partial, target_queries)
    shares = call(
        project_out_kernel,
        shape(4, quarter // 4, D),
        core_info,
        partial.reshape(8, 4, quarter + 16, 128),
        output_weight,
        out_mine,
        out_theirs,
        specs=[SMEM, VMEM] + [ANY] * 3,
        scratch=[pltpu.VMEM((quarter, 512), BF16), pltpu.VMEM((512, D), BF16), DMA((7,))],
        limit=62.5,
        flops=2 * quarter * 512 * D,
    )
    shares = exchange(shares, "zh")
    shares, mine = together(shares, mine)
    theirs = swapped(mine, "c", 2, 1)
    first = at["x"] * quarter + at["zh"] * (quarter // 4)
    own_source = lax.dynamic_slice_in_dim(source_full, first, quarter // 4, 1)
    encoder_rows = call(
        residual_kernel, shape(4, quarter // 4, D), shares, own_source, specs=[VMEM] * 2
    )
    encoder_rows = exchange(encoder_rows, "zh").reshape(quarter, D)
    memory = call(
        memory_kernel,
        shape(4, 4, 2, quarter, 128),
        core_info,
        encoder_rows,
        gains[1],
        mine,
        theirs,
        specs=[SMEM, ANY, VMEM, ANY, ANY],
        scratch=[
            pltpu.VMEM((quarter, D), BF16),
            pltpu.VMEM((quarter, D), BF16),
            pltpu.VMEM((4, D, 256), BF16),
            DMA((16,)),
            DMA((1,)),
        ],
        limit=63,
        flops=2 * quarter * D * 1024,
    )
    encoder_full = lax.all_gather(encoder_rows, "x", axis=0, tiled=True)

    target_queries = lax.all_gather(target_queries, QUERY_GROUP, axis=0)
    memory = exchange(memory.reshape(16, 2, quarter, 128), ("yh", "x")).reshape(4, 4, 2, quarter, 128)
    crossed = attend(
        target_queries, [memory], [(0, (k // 4, k % 4)) for k in range(16)], memory_info, target_rows, True
    )
    crossed, encoder_full = together(crossed, encoder_full)
    crossed = exchange(crossed.reshape(8, target_rows + 16, 128), QUERY_GROUP)
    head_at = at["zh"] * 4 + at["x"]
    encoder_out = lax.dynamic_slice_in_dim(encoder_full, head_at * 128, 128, 1)
    cross_context = call(
        finish_kernel, shape(target_rows, 128), target_info, crossed, specs=[SMEM, VMEM]
    )
    return (encoder_out, cross_context)


def solution(mesh):
    fine = Mesh(mesh.devices.reshape([size for _, size in AXES]), [name for name, _ in AXES])
    columns = P(None, HEAD)
    in_specs = (
        P(SEQ, HEAD),
        P(SEQ, HEAD),
        P(),
        P(),
        P(),
        columns,
        columns,
        columns,
        P(HEAD, None),
        P(),
        columns,
        columns,
        columns,
        P(),
    )
    out_specs = (P(SEQ, HEAD), P(SEQ, HEAD))
    return jax.shard_map(shards, mesh=fine, in_specs=in_specs, out_specs=out_specs, check_vma=False)
```

```python
import functools
import math

import jax
import jax.numpy as jnp
from jax import lax
from jax.experimental import pallas as pl
from jax.experimental.pallas import tpu as pltpu
from jax.sharding import Mesh, PartitionSpec as P

HD = 128
D = 2048
EPSILON = 1e-05
MASKED = -1e30
SCORE_SCALE = HD ** (-0.5) * math.log2(math.e)
F32 = jnp.float32
BF16 = jnp.bfloat16

AXES = (("zl", 2), ("yh", 4), ("yl", 2), ("c", 2), ("zh", 4), ("x", 4))
SEQ = ("zl", "yh", "yl", "c")
HEAD = ("zh", "x")
QUERY_GROUP = ("zl", "yl", "c")
VMEM = pl.BlockSpec(memory_space=pltpu.VMEM)
SMEM = pl.BlockSpec(memory_space=pltpu.SMEM)
ANY = pl.BlockSpec(memory_space=pl.ANY)
HBM = pl.BlockSpec(memory_space=pltpu.HBM)
DMA = pltpu.SemaphoreType.DMA


def call(kernel, out_shape, *args, specs, out=None, scratch=(), limit=48, flops=0, transcendentals=0):
    outs = jax.tree.leaves(out_shape)
    size = sum(math.prod(a.shape) * a.dtype.itemsize for a in (*args, *outs))
    return pl.pallas_call(
        kernel,
        out_shape=out_shape,
        in_specs=specs,
        out_specs=jax.tree.map(lambda _: VMEM, out_shape) if out is None else out,
        scratch_shapes=scratch,
        compiler_params=pltpu.CompilerParams(vmem_limit_bytes=int(limit * 1024 * 1024)),
        cost_estimate=pl.CostEstimate(flops=flops, bytes_accessed=size, transcendentals=transcendentals),
    )(*args)


def shape(*dims, dtype=BF16):
    return jax.ShapeDtypeStruct(dims, dtype)


def started(pairs, sems):
    copies = [pltpu.make_async_copy(a, b, sems.at[i]) for i, (a, b) in enumerate(pairs)]
    for copy in copies:
        copy.start()
    return copies


def wait_for(copies):
    for copy in copies:
        copy.wait()


def repeat_kernel(x_ref, out_ref, sems):
    wait_for(started([(x_ref, out_ref.at[i]) for i in range(out_ref.shape[0])], sems))


def repeated(x, times):
    return call(
        repeat_kernel, shape(times, *x.shape), x, specs=[VMEM], out=HBM, scratch=[DMA((times,))], limit=63.9
    )


def normed_rows(pieces, gains):
    total = functools.reduce(jnp.add, pieces)
    mean = jnp.sum(total, axis=-1, keepdims=True) * (1.0 / D)
    centers = [p - mean for p in pieces]
    squares = functools.reduce(jnp.add, [c * c for c in centers])
    spread = jnp.sum(squares, axis=-1, keepdims=True) * (1.0 / D)
    inverse = lax.rsqrt(spread + EPSILON)
    return [(c * inverse * g).astype(BF16) for c, g in zip(centers, gains)]


def norm_gathered(x_ref, gain_ref, norm_ref, step=64):
    rows = x_ref.shape[1]

    def body(i, _):
        r = pl.multiple_of(i * step, step)
        pieces = [x_ref[j, pl.ds(r, step), :].astype(F32) for j in range(16)]
        gains = [gain_ref[:, j * 128 : (j + 1) * 128] for j in range(16)]
        for j, n in enumerate(normed_rows(pieces, gains)):
            norm_ref[pl.ds(r, step), j * 128 : (j + 1) * 128] = n
        return 0

    lax.fori_loop(0, rows // step, body, 0)


def qkv_kernel(x_ref, gain_ref, wq_ref, wk_ref, wv_ref, q_ref, kv_ref, norm_ref, w_ref, q_one_ref, in_sems, out_sems):
    weights = started(
        [(w, w_ref.at[:, i * 128 : (i + 1) * 128]) for i, w in enumerate((wq_ref, wk_ref, wv_ref))], in_sems
    )
    norm_gathered(x_ref, gain_ref, norm_ref)
    wait_for(weights)
    out = jnp.dot(norm_ref[...], w_ref[...], preferred_element_type=F32)
    q_one_ref[...] = (out[:, :128] * SCORE_SCALE).astype(BF16)
    copies = started([(q_one_ref, q_ref.at[a]) for a in range(q_ref.shape[0])], out_sems)
    kv_ref[0] = out[:, 128:256].astype(BF16)
    kv_ref[1] = out[:, 256:].astype(BF16)
    wait_for(copies)


def target_kernel(x_ref, gain_ref, wq_ref, q_ref, norm_ref, x_vmem, w_ref, x_sems, w_sem):
    rows = x_ref.shape[1]
    parts = x_vmem.shape[0]
    step = rows // parts
    weights = started([(wq_ref, w_ref)], w_sem)
    pieces = started(
        [(x_ref.at[:, i * step : (i + 1) * step, :], x_vmem.at[i]) for i in range(parts)], x_sems
    )
    for i, piece in enumerate(pieces):
        piece.wait()
        norm_gathered(x_vmem.at[i], gain_ref, norm_ref.at[i * step : (i + 1) * step, :])
    wait_for(weights)
    out = jnp.dot(norm_ref[...], w_ref[...], preferred_element_type=F32)
    q_ref[...] = (out * SCORE_SCALE).astype(BF16)


def attend_kernel(part, blocks, fetched, info_ref, q_ref, *refs):
    kv_refs, (out_ref, ka_ref, va_ref, *q_scratch) = refs[: len(refs) - 3 - fetched * 2], refs[len(refs) - 3 - fetched * 2 :]
    members, rows, _ = q_ref.shape
    q_vmem, q_copy = q_ref, []
    if fetched:
        q_vmem, q_sem = q_scratch
        q_copy = started([(q_ref, q_vmem)], q_sem)
    limit = info_ref[0]
    n = kv_refs[0].shape[-2]
    lane = lax.broadcasted_iota(jnp.int32, (n, 128), 1)
    row = lax.broadcasted_iota(jnp.int32, (n, 128), 0)
    for b, (ref, at) in enumerate(blocks):
        place = info_ref[1 + b] + row
        bias = jnp.where((lane == 0) & (place >= limit), MASKED, 0.0).astype(BF16)
        here = slice(b * n, (b + 1) * n)
        ka_ref[here, :128] = kv_refs[ref][(*at, 0)]
        ka_ref[here, 128:] = bias
        va_ref[here, :128] = kv_refs[ref][(*at, 1)]
        va_ref[here, 128:] = jnp.ones((n, 128), BF16)
    ones = jnp.where(lax.broadcasted_iota(jnp.int32, (256, 128), 1) == 0, 1.0, 0.0).astype(BF16)
    group = min(part, 128)
    groups = part // group
    eye = lax.broadcasted_iota(jnp.int32, (group, 128), 0) == lax.broadcasted_iota(jnp.int32, (group, 128), 1)
    block = 256
    each = rows // block
    unroll = 8

    wait_for(q_copy)

    def body(i, _):
        for u in range(unroll):
            step = i * unroll + u
            a, r = (step, 0) if each == 1 else (step // each, (u % each) * block)
            q = jnp.concatenate([q_vmem[a, pl.ds(r, block), :], ones], axis=1)
            scores = lax.dot_general(q, ka_ref[...], (((1,), (1,)), ((), ())), preferred_element_type=F32)
            top = jnp.max(scores, axis=1, keepdims=True)
            weights = jnp.exp2(scores - top).astype(BF16)
            summed = jnp.dot(weights, va_ref[...], preferred_element_type=F32)
            denominator = summed[:, 128:]
            context = (summed[:, :128] / denominator).astype(BF16)
            level = top + jnp.log2(denominator)
            for g in range(block // group):
                at = r + g * group
                p, inside = at // part, at % part
                out_ref[a, p, inside : inside + group, :] = context[g * group : (g + 1) * group]
                line = jnp.sum(jnp.where(eye, level[g * group : (g + 1) * group], 0.0), axis=0, keepdims=True)
                stat_ref_store(out_ref, a, p, part, inside // group, groups, line)
        return 0

    lax.fori_loop(0, members * each // unroll, body, 0)


def stat_ref_store(out_ref, a, p, part, g, groups, line):
    high = line.astype(BF16)
    rest = line - high.astype(F32)
    middle = rest.astype(BF16)
    low = (rest - middle.astype(F32)).astype(BF16)
    out_ref[a, p, part + g : part + g + 1, :] = high
    out_ref[a, p, part + groups + g : part + groups + g + 1, :] = middle
    out_ref[a, p, part + 2 * groups + g : part + 2 * groups + g + 1, :] = low


def mixing(levels):
    top = functools.reduce(jnp.maximum, levels)
    raw = [jnp.exp2(v - top) for v in levels]
    total = functools.reduce(jnp.add, raw)
    return [v / total for v in raw]


def combined(read_rows, read_stats, members, part):
    group = min(part, 128)
    groups = part // group
    eye = lax.broadcasted_iota(jnp.int32, (group, 128), 0) == lax.broadcasted_iota(jnp.int32, (group, 128), 1)
    levels = []
    for a in range(members):
        stats = read_stats(a).astype(F32)
        levels.append(stats[:groups] + stats[groups : 2 * groups] + stats[2 * groups : 3 * groups])
    shares = mixing(levels)
    out = []
    for g in range(groups):
        total = None
        for a in range(members):
            column = jnp.sum(jnp.where(eye, shares[a][g : g + 1], 0.0), axis=1, keepdims=True)
            term = read_rows(a)[g * group : (g + 1) * group].astype(F32) * column
            total = term if total is None else total + term
        out.append(total)
    return out


def project_out_kernel(info_ref, r_ref, own_ref, mine_ref, theirs_ref, out_ref, ctx_ref, w_ref, sems):
    core = info_ref[0]
    half = D // 2
    copies = started(
        [(own_ref, w_ref.at[:128])]
        + [
            (ref.at[k], w_ref.at[(k + 1) * 128 : (k + 2) * 128, pl.ds(pl.multiple_of(first * half, half), half)])
            for ref, first in ((mine_ref, core), (theirs_ref, 1 - core))
            for k in range(3)
        ],
        sems,
    )
    members, _, full, _ = r_ref.shape
    part = full - 16
    for k in range(4):
        h = info_ref[1 + k]
        pieces = combined(
            lambda a: r_ref[a, h, :part, :], lambda a: r_ref[a, h, part:, :], members, part
        )
        ctx_ref[:, k * 128 : (k + 1) * 128] = pieces[0].astype(BF16)
    wait_for(copies)
    out = jnp.dot(ctx_ref[...], w_ref[...], preferred_element_type=F32).astype(BF16)
    for z in range(4):
        out_ref[z] = out[z * 16 : (z + 1) * 16]


def residual_kernel(r_ref, s_ref, out_ref):
    for j in range(16):
        cols = slice(j * 128, (j + 1) * 128)
        total = s_ref[j].astype(F32)
        for z in range(4):
            total = total + r_ref[z, :, cols].astype(F32)
        total = total.astype(BF16)
        for z in range(4):
            out_ref[z, :, cols] = total


def memory_kernel(info_ref, e_ref, gain_ref, mine_ref, theirs_ref, kv_ref, norm_ref, e_vmem, w_ref, sems, e_sem):
    core = info_ref[0]
    half = D // 2
    rows = started([(e_ref, e_vmem)], e_sem)
    copies = started(
        [
            (ref.at[h, t], w_ref.at[h, pl.ds(pl.multiple_of(first * half, half), half), t * 128 : (t + 1) * 128])
            for h in range(4)
            for ref, first in ((mine_ref, core), (theirs_ref, 1 - core))
            for t in range(2)
        ],
        sems,
    )
    wait_for(rows)
    pieces = [e_vmem[:, j * 128 : (j + 1) * 128].astype(F32) for j in range(16)]
    gains = [gain_ref[:, j * 128 : (j + 1) * 128] for j in range(16)]
    for j, n in enumerate(normed_rows(pieces, gains)):
        norm_ref[:, j * 128 : (j + 1) * 128] = n
    for h in range(4):
        wait_for(copies[h * 4 : (h + 1) * 4])
        out = jnp.dot(norm_ref[...], w_ref[h], preferred_element_type=F32).astype(BF16)
        for b in range(4):
            kv_ref[b, h, 0] = out[:, :128]
            kv_ref[b, h, 1] = out[:, 128:]


def finish_kernel(info_ref, r_ref, out_ref):
    members, full, _ = r_ref.shape
    part = full - 16
    pieces = combined(lambda a: r_ref[a, :part, :], lambda a: r_ref[a, part:, :], members, part)
    first, limit = info_ref[0], info_ref[1]
    for g, piece in enumerate(pieces):
        n = piece.shape[0]
        place = first + g * n + lax.broadcasted_iota(jnp.int32, (n, 128), 0)
        out_ref[g * n : (g + 1) * n, :] = jnp.where(place < limit, piece, 0.0).astype(BF16)


def exchange(x, axes):
    return lax.all_to_all(x, axes, 0, 0, tiled=True)


def attend(q, kvs, blocks, info, part, fetched):
    members, rows, _ = q.shape
    keys = len(blocks) * kvs[0].shape[-2]
    return call(
        functools.partial(attend_kernel, part, blocks, fetched),
        shape(members, rows // part, part + 16, 128),
        info,
        q,
        *kvs,
        specs=[SMEM, ANY if fetched else VMEM] + [VMEM] * len(kvs),
        scratch=[pltpu.VMEM((keys, 256), BF16), pltpu.VMEM((keys, 256), BF16)]
        + ([pltpu.VMEM(q.shape, BF16), DMA((1,))] if fetched else []),
        limit=62 if fetched else 48,
        flops=4 * members * rows * keys * 256,
        transcendentals=members * rows * keys,
    )


def swapped(x, axis, size, by):
    return lax.ppermute(x, axis, [(i, i ^ by) for i in range(size)])


def together(*arrays):
    return lax.optimization_barrier(arrays)


def shards(
    source_hidden,
    target_hidden,
    source_length,
    target_length,
    encoder_gain,
    query_weight,
    key_weight,
    value_weight,
    output_weight,
    final_gain,
    cross_query,
    cross_key,
    cross_value,
    cross_gain,
):
    rows = source_hidden.shape[0]
    target_rows = target_hidden.shape[0]
    at = {name: lax.axis_index(name) for name, _ in AXES}
    seq_at = ((at["zl"] * 4 + at["yh"]) * 2 + at["yl"]) * 2 + at["c"]
    quarter = rows // 4
    core_info = jnp.stack([at["c"], at["x"], at["x"] ^ 1, at["x"] ^ 3, at["x"] ^ 2])

    def first_of(yh):
        return (((at["zl"] * 4 + yh) * 2 + at["yl"]) * 2 + at["c"]) * rows

    key_info = jnp.stack([source_length[0]] + [first_of(at["yh"] ^ k) for k in range(4)])
    memory_info = jnp.stack(
        [source_length[0]] + [first_of(k // 4) + (k % 4) * quarter for k in range(16)]
    )
    target_info = jnp.stack([seq_at * target_rows, target_length[0]])
    gains = [g.reshape(1, D) for g in (encoder_gain, final_gain, cross_gain)]

    half = at["c"] * (D // 2)
    out_half = lax.dynamic_slice_in_dim(output_weight, half, D // 2, 1)
    out_halves = [swapped(out_half, "x", 4, k) for k in (1, 3)]
    target_full = lax.all_gather(target_hidden, HEAD, axis=0)
    source_full = exchange(repeated(source_hidden, 16), HEAD)
    source_full, *out_halves = together(source_full, *out_halves)
    half_weights = jnp.stack([lax.dynamic_slice_in_dim(w, half, D // 2, 0) for w in (cross_key, cross_value)])
    source_full, half_weights = together(source_full, half_weights)
    mine = lax.all_gather(half_weights, "x", axis=0)

    queries, keys_values = call(
        qkv_kernel,
        (shape(8, rows, 128), shape(2, rows, 128)),
        source_full,
        gains[0],
        query_weight,
        key_weight,
        value_weight,
        specs=[VMEM, VMEM, ANY, ANY, ANY],
        out=(HBM, VMEM),
        scratch=[
            pltpu.VMEM((rows, D), BF16),
            pltpu.VMEM((D, 384), BF16),
            pltpu.VMEM((rows, 128), BF16),
            DMA((3,)),
            DMA((8,)),
        ],
        flops=2 * rows * D * 384,
    )
    key_sets = [keys_values] + [swapped(keys_values, "yh", 4, k) for k in (1, 2, 3)]
    queries = exchange(queries, QUERY_GROUP)
    queries, *out_halves = together(queries, *out_halves)
    out_halves.append(swapped(out_halves[0], "x", 4, 3))
    partial = attend(queries, key_sets, [(k, ()) for k in range(4)], key_info, quarter, False)
    partial, *out_halves = together(partial, *out_halves)
    out_mine = jnp.stack(out_halves)
    out_theirs = swapped(out_mine, "c", 2, 1)
    partial = exchange(partial.reshape(32, rows // 4 + 16, 128), QUERY_GROUP + ("x",))
    target_queries = call(
        target_kernel,
        shape(target_rows, 128),
        target_full,
        gains[2],
        cross_query,
        specs=[ANY, VMEM, ANY],
        scratch=[
            pltpu.VMEM((target_rows, D), BF16),
            pltpu.VMEM((4, 16, target_rows // 4, 128), BF16),
            pltpu.VMEM((D, 128), BF16),
            DMA((4,)),
            DMA((1,)),
        ],
        flops=2 * target_rows * D * 128,
    )
    partial, target_queries = together(partial, target_queries)
    shares = call(
        project_out_kernel,
        shape(4, quarter // 4, D),
        core_info,
        partial.reshape(8, 4, quarter + 16, 128),
        output_weight,
        out_mine,
        out_theirs,
        specs=[SMEM, VMEM] + [ANY] * 3,
        scratch=[pltpu.VMEM((quarter, 512), BF16), pltpu.VMEM((512, D), BF16), DMA((7,))],
        limit=62.5,
        flops=2 * quarter * 512 * D,
    )
    shares = exchange(shares, "zh")
    shares, mine = together(shares, mine)
    theirs = swapped(mine, "c", 2, 1)
    first = at["x"] * quarter + at["zh"] * (quarter // 4)
    own_source = lax.dynamic_slice_in_dim(source_full, first, quarter // 4, 1)
    encoder_rows = call(
        residual_kernel, shape(4, quarter // 4, D), shares, own_source, specs=[VMEM] * 2
    )
    encoder_rows = exchange(encoder_rows, "zh").reshape(quarter, D)
    memory = call(
        memory_kernel,
        shape(4, 4, 2, quarter, 128),
        core_info,
        encoder_rows,
        gains[1],
        mine,
        theirs,
        specs=[SMEM, ANY, VMEM, ANY, ANY],
        scratch=[
            pltpu.VMEM((quarter, D), BF16),
            pltpu.VMEM((quarter, D), BF16),
            pltpu.VMEM((4, D, 256), BF16),
            DMA((16,)),
            DMA((1,)),
        ],
        limit=63,
        flops=2 * quarter * D * 1024,
    )
    encoder_full = lax.all_gather(encoder_rows, "x", axis=0, tiled=True)

    target_queries = lax.all_gather(target_queries, QUERY_GROUP, axis=0)
    memory = exchange(memory.reshape(16, 2, quarter, 128), ("yh", "x")).reshape(4, 4, 2, quarter, 128)
    crossed = attend(
        target_queries, [memory], [(0, (k // 4, k % 4)) for k in range(16)], memory_info, target_rows, True
    )
    crossed, encoder_full = together(crossed, encoder_full)
    crossed = exchange(crossed.reshape(8, target_rows + 16, 128), QUERY_GROUP)
    head_at = at["zh"] * 4 + at["x"]
    encoder_out = lax.dynamic_slice_in_dim(encoder_full, head_at * 128, 128, 1)
    cross_context = call(
        finish_kernel, shape(target_rows, 128), target_info, crossed, specs=[SMEM, VMEM]
    )
    return (encoder_out, cross_context)


def solution(mesh):
    fine = Mesh(mesh.devices.reshape([size for _, size in AXES]), [name for name, _ in AXES])
    columns = P(None, HEAD)
    in_specs = (
        P(SEQ, HEAD),
        P(SEQ, HEAD),
        P(),
        P(),
        P(),
        columns,
        columns,
        columns,
        P(HEAD, None),
        P(),
        columns,
        columns,
        columns,
        P(),
    )
    out_specs = (P(SEQ, HEAD), P(SEQ, HEAD))
    return jax.shard_map(shards, mesh=fine, in_specs=in_specs, out_specs=out_specs, check_vma=False)
```
